32 devices in a mesh: row: 8 (over z, core), col: 2 (over x), vec: 2 (over y).
Axes of the slice: x: 2, y: 2, z: 4, core: 2. Of those that a mesh axis runs over, the one named last changes fastest.
Arguments:
- vectors: bfloat16 [16, 16384], P('vec', ('row', 'col')), may hold values from -6 to 6
- tile_vals: bfloat16 [8, 2, 256, 128, 128], P('row', 'col'), may hold values from -0.09375 to 0.09375
- tile_rows: int32 [8, 2, 256], P('row', 'col'), may hold values from 0 to 127, as said below
- tile_cols: int32 [8, 2, 256], P('row', 'col'), may hold values from 0 to 127, as said below
- tile_counts: int32 [8, 2], P('row', 'col'), may hold values from 1 to 256, as said below
Outputs:
- product: bfloat16 [16, 16384], P('vec', ('row', 'col'))
- gram: float32 [16, 16], P(None, 'vec')
The draws below stay inside these ranges and needn't reach their ends.
Inputs may be any that keep to these rules, and one draw needn't show every extreme that they name: `tile_rows`: list [i, j] names tiles whose row index r has i * 16 <= r < (i + 1) * 16 and whose column index c has (c // 8) % (2) == j, that is the column's block of 8 tile rows, numbered c // 8, is held by column group j; live slots name distinct tiles with r >= c; slots at or beyond the count hold in-range indices that must be ignored. `tile_cols`: see tile_rows; the same slots. `tile_counts`: some lists are full in every draw; lists near the top of the triangle hold few tiles.
All inputs are finite; a program needn't handle non-finite values.
Results may differ from the reference program's by a relative error of at most 0.001.
Values may be sent and summed in bfloat16 or wider, within the bound.
No kernel may reach another device: no remote copies, remote signals or barrier semaphores. Data moves between devices by JAX's collectives and lax.ppermute only.
A program may use at most 64 MiB of HBM per device.

```python
import math
import jax
import jax.numpy as jnp
from jax import lax

V = 16
TILE = 128
CH = 8
CAP = 256
NDIM = 16384
N_ROW = 8
N_COL = 2


def layout_lists(key):
    span = N_COL * CH
    full = span * N_ROW * CH
    place = jnp.arange(full, dtype=jnp.int32)
    inner = place // (N_ROW * CH)
    rest = place % (N_ROW * CH)
    group = rest // CH
    offset = rest % CH
    dev_i = jnp.arange(N_ROW, dtype=jnp.int32)[:, None, None]
    dev_j = jnp.arange(N_COL, dtype=jnp.int32)[None, :, None]
    rows = dev_i * span + inner[None, None, :] + 0 * dev_j
    cols = group[None, None, :] * span + dev_j * CH + offset[None, None, :] + 0 * dev_i
    valid = rows >= cols
    noise = jax.random.randint(jax.random.fold_in(key, 11), (N_ROW, N_COL, full), 0, 2 ** 17)
    score = jnp.where(valid, noise * full + place[None, None, :], -1)
    _, picked = lax.top_k(score, CAP)
    pick_rows = jnp.take_along_axis(rows, picked, axis=2).astype(jnp.int32)
    pick_cols = jnp.take_along_axis(cols, picked, axis=2).astype(jnp.int32)
    nvalid = jnp.sum(valid.astype(jnp.int32), axis=2)
    jitter = jax.random.randint(jax.random.fold_in(key, 12), (N_ROW, N_COL), 0, 4)
    counts = jnp.clip(nvalid * CAP * 3 // 2 // full - jitter, 1, CAP).astype(jnp.int32)
    return (pick_rows, pick_cols, counts)


def draw_tile_rows(key, part):
    return layout_lists(key)[0]


def draw_tile_cols(key, part):
    return layout_lists(key)[1]


def draw_tile_counts(key, part):
    return layout_lists(key)[2]


def level_of(rng, shape, split, low, high):
    loudness = 1.0
    for position, blocks in split:
        steps = jax.random.uniform(jax.random.fold_in(jax.random.fold_in(rng, 6), position), (blocks,), jnp.float32, low / len(split), high / len(split))
        loudness = loudness * jnp.repeat(jnp.exp(steps), shape[position] // blocks).reshape((-1,) + (1,) * (len(shape) - 1 - position))
    return loudness


def scatter_about(key, extent, spread, limit, shards=(), kind=jnp.bfloat16):
    drawn = spread * jax.random.normal(key, extent, jnp.float32)
    if shards:
        drawn = drawn * level_of(key, extent, shards, -0.22, 0.18)
    return jnp.clip(drawn, -limit, limit).astype(kind)


def setup_inputs(seed: int = 0) -> dict:
    splits = jax.random.split(jax.random.key(seed), 6)
    vectors = scatter_about(splits[0], (V, NDIM), 1.0, 6.0, ((0, 2), (1, 16)))
    tile_vals = scatter_about(splits[1], (N_ROW, N_COL, CAP, TILE, TILE), (TILE * CAP // CH) ** -0.5, 0.09375, ((0, 8), (1, 2)))
    tile_rows = draw_tile_rows(jax.random.fold_in(splits[5], 71), 0)
    tile_cols = draw_tile_cols(jax.random.fold_in(splits[5], 71), 0)
    tile_counts = draw_tile_counts(jax.random.fold_in(splits[5], 71), 0)
    return {"vectors": vectors, "tile_vals": tile_vals, "tile_rows": tile_rows, "tile_cols": tile_cols, "tile_counts": tile_counts}


def reference(vectors, tile_vals, tile_rows, tile_cols, tile_counts):
    vcount, ndim = vectors.shape
    tile = tile_vals.shape[-1]
    slots = tile_vals.shape[2]
    ntiles = ndim // tile
    blocks = vectors.astype(jnp.float32).reshape(vcount, ntiles, tile).transpose(1, 0, 2)
    flat_vals = tile_vals.reshape(-1, slots, tile, tile)
    flat_rows = tile_rows.reshape(-1, slots).astype(jnp.int32)
    flat_cols = tile_cols.reshape(-1, slots).astype(jnp.int32)
    flat_counts = tile_counts.reshape(-1).astype(jnp.int32)

    def step(total, item):
        vals, rows, cols, count = item
        live = jnp.arange(slots, dtype=jnp.int32) < count
        mirror = live & (rows != cols)
        vals32 = vals.astype(jnp.float32)
        down = jnp.einsum('tij,tvj->tvi', vals32, blocks[cols], precision=lax.Precision.HIGHEST)
        upper = jnp.einsum('tij,tvi->tvj', vals32, blocks[rows], precision=lax.Precision.HIGHEST)
        down = down * live.astype(jnp.float32)[:, None, None]
        upper = upper * mirror.astype(jnp.float32)[:, None, None]
        total = total.at[rows].add(down).at[cols].add(upper)
        return (total, None)
    start = jnp.zeros((ntiles, vcount, tile), jnp.float32)
    total, _ = lax.scan(step, start, (flat_vals, flat_rows, flat_cols, flat_counts))
    image = total.transpose(1, 0, 2).reshape(vcount, ndim)
    gram = jnp.dot(vectors.astype(jnp.float32), image.T, precision=lax.Precision.HIGHEST) / math.sqrt(ndim)
    return (image.astype(jnp.bfloat16), gram)
```

```python
import functools
import math

import jax
import jax.numpy as jnp
from jax import lax
from jax.experimental import pallas as pl
from jax.experimental.pallas import tpu as pltpu
from jax.sharding import PartitionSpec as P

CHUNK = 64
GROUP = 8
SMEM = pl.BlockSpec(memory_space=pltpu.SMEM)
VMEM = pl.BlockSpec(memory_space=pltpu.VMEM)
F32 = jnp.float32
HIGHEST = lax.Precision.HIGHEST


def params(mib):
    return pltpu.CompilerParams(vmem_limit_bytes=mib * 2**20)


def place_block(low, high, block, first, stretch, tile):
    vlocal = block.shape[0]
    zero = jnp.zeros((vlocal, tile), block.dtype)
    for q in range(stretch):
        part = block[:, q * tile : (q + 1) * tile]
        low[first + q] = jnp.concatenate([part, zero], axis=0)
        high[first + q] = jnp.concatenate([zero, part], axis=0)


def multiply_tiles(pick, forward, count, tiles, low, high, sums):
    slots = tiles.shape[0]
    tile = tiles.shape[-1]
    vlocal = sums[0].shape[1]
    for acc in sums:
        acc[...] = jnp.zeros_like(acc)

    def chunk(step, carry):
        for g in range(CHUNK // (2 * GROUP)):
            results = []
            for u in range(GROUP):
                s = step * CHUNK + g * 2 * GROUP + 2 * u
                in0, out0 = pick(s)
                in1, out1 = pick(s + 1)
                left = jnp.concatenate([low[in0], high[in1]], axis=1)
                if forward:
                    right = jnp.concatenate([tiles[s], tiles[s + 1]], axis=1)
                    dims = (((1,), (1,)), ((), ()))
                else:
                    right = tiles[pl.ds(s, 2)].reshape(2 * tile, tile)
                    dims = (((1,), (0,)), ((), ()))
                both = lax.dot_general(left, right, dims, preferred_element_type=F32)
                results.append((both, out0, out1))
            for u, (both, out0, out1) in enumerate(results):
                a, b = sums[(2 * u) % len(sums)], sums[(2 * u + 1) % len(sums)]
                a[out0] += both[:vlocal]
                b[out1] += both[vlocal:]
        return carry

    assert slots % CHUNK == 0
    lax.fori_loop(0, pl.cdiv(count, CHUNK), chunk, 0)


def places(rows, cols, span, stretch):
    def get(s):
        r, c = rows[s], cols[s]
        return r, c, lax.rem(r, span), lax.div(c, span) * stretch + lax.rem(c, stretch)

    return get


def mirror_kernel(sizes, pos, rows, cols, counts, tiles, *refs):
    nz, ncol, stretch = sizes
    span = ncol * stretch
    blocks, (mine, other), (low, high, *sums) = refs[:ncol], refs[ncol : ncol + 2], refs[ncol + 2 :]
    tile = tiles.shape[-1]
    width = stretch * tile
    count = counts[0]
    z, core, j = pos[0], pos[1], pos[2]
    for t in range(ncol):
        place_block(low, high, blocks[t], lax.rem(j + ncol - t, ncol) * stretch, stretch, tile)
    low[span] = jnp.zeros(low.shape[1:], low.dtype)
    high[span] = jnp.zeros(high.shape[1:], high.dtype)
    get = places(rows, cols, span, stretch)

    def pick(s):
        r, c, row_place, col_place = get(s)
        return jnp.where((s < count) & (r != c), row_place, span), col_place

    multiply_tiles(pick, False, count, tiles, low, high, sums)
    for s in range(nz):
        target = 2 * lax.rem(z + s, nz)
        for out, c in ((mine, core), (other, 1 - core)):
            for q in range(stretch):
                at = (target + c) * stretch + q
                total = sums[0][at]
                for acc in sums[1:]:
                    total += acc[at]
                out[:, s * width + q * tile : s * width + (q + 1) * tile] = total


def forward_kernel(sizes, pos, rows, cols, counts, tiles, near, far, *refs):
    nz, ncol, stretch = sizes
    span = ncol * stretch
    outs, (low, high, *sums) = refs[:ncol], refs[ncol:]
    tile = tiles.shape[-1]
    width = stretch * tile
    count = counts[0]
    z, core, j = pos[0], pos[1], pos[2]
    for s in range(nz):
        source = 2 * lax.rem(z + nz - s, nz)
        for ref, c in ((near, core), (far, 1 - core)):
            place_block(low, high, ref[:, s * width : (s + 1) * width], (source + c) * stretch, stretch, tile)
    dead = 2 * nz * stretch
    low[dead] = jnp.zeros(low.shape[1:], low.dtype)
    high[dead] = jnp.zeros(high.shape[1:], high.dtype)
    get = places(rows, cols, span, stretch)

    def pick(s):
        _, _, row_place, col_place = get(s)
        return jnp.where(s < count, col_place, dead), row_place

    multiply_tiles(pick, True, count, tiles, low, high, sums)
    for t in range(ncol):
        first = lax.rem(j + t, ncol) * stretch
        for q in range(stretch):
            total = sums[0][first + q]
            for acc in sums[1:]:
                total += acc[first + q]
            outs[t][:, q * tile : (q + 1) * tile] = total


def pair_kernel(nz, mine, theirs, *outs):
    width = mine.shape[1] // nz
    for s in range(nz):
        at = slice(s * width, (s + 1) * width)
        outs[s][...] = mine[:, at] + theirs[:, at]


def gram_kernel(nz, ncol, nvec, *refs):
    cols, refs = refs[:nz], refs[nz:]
    parts, refs = refs[:ncol], refs[ncol:]
    xs, (image, share) = refs[: nvec * ncol], refs[nvec * ncol :]
    total = parts[0][...]
    for ref in cols:
        total += ref[...]
    image[...] = total
    terms = [total] + [ref[...] for ref in parts[1:]]
    for k in range(nvec):
        product = None
        for t in range(ncol):
            one = lax.dot_general(
                xs[k * ncol + t][...].astype(F32),
                terms[t],
                (((1,), (1,)), ((), ())),
                precision=HIGHEST,
                preferred_element_type=F32,
            )
            product = one if product is None else product + one
        share[k] = product


def shards(sizes, vectors, tile_vals, tile_rows, tile_cols, tile_counts):
    nz, ncol, nvec = sizes
    nrow = 2 * nz
    vlocal, width = vectors.shape
    slots, tile = tile_vals.shape[2], tile_vals.shape[-1]
    stretch = width // tile
    span = ncol * stretch
    tiles, rows, cols, counts = tile_vals[0, 0], tile_rows[0, 0], tile_cols[0, 0], tile_counts[0]
    i, j, k = lax.axis_index("row"), lax.axis_index("col"), lax.axis_index("vec")
    pos = jnp.stack([i // 2, i % 2, j]).astype(jnp.int32)

    def core_swap(x):
        return lax.ppermute(x, "row", [(a, a ^ 1) for a in range(nrow)])

    def z_shift(x, s):
        return lax.ppermute(x, "row", [(a, (a + 2 * s) % nrow) for a in range(nrow)])

    def col_shift(x, t):
        return lax.ppermute(x, "col", [(a, (a + t) % ncol) for a in range(ncol)])

    def vec_shift(x, t):
        return lax.ppermute(x, "vec", [(a, (a + t) % nvec) for a in range(nvec)])

    row_x = [vectors] + [col_shift(vectors, t) for t in range(1, ncol)]
    near = jnp.concatenate([vectors] + [z_shift(vectors, s) for s in range(1, nz)], axis=1)
    far = core_swap(near)

    def tables(count):
        shape = pltpu.VMEM((count + 1, 2 * vlocal, tile), vectors.dtype)
        return [shape, shape]

    def sums(count):
        return [pltpu.VMEM((count, vlocal, tile), F32)] * 2

    block = jax.ShapeDtypeStruct((vlocal, width), F32)
    ring = jax.ShapeDtypeStruct((vlocal, nz * width), F32)
    step = (nz, ncol, stretch)
    cost = pl.CostEstimate(
        flops=2 * slots * tile * tile * 2 * vlocal, bytes_accessed=slots * tile * tile * 2, transcendentals=0
    )
    mine, other = pl.pallas_call(
        functools.partial(mirror_kernel, step),
        out_shape=[ring, ring],
        in_specs=[SMEM] * 4 + [VMEM] * (1 + ncol),
        out_specs=[VMEM] * 2,
        scratch_shapes=tables(span) + sums(nrow * stretch),
        compiler_params=params(24),
        cost_estimate=cost,
        name="mirror",
    )(pos, rows, cols, counts, tiles, *row_x)
    theirs = core_swap(other)
    pieces = pl.pallas_call(
        functools.partial(pair_kernel, nz),
        out_shape=[block] * nz,
        in_specs=[VMEM] * 2,
        out_specs=[VMEM] * nz,
        compiler_params=params(8),
        name="pair",
    )(mine, theirs)
    col_parts = [pieces[0]] + [z_shift(pieces[s], s) for s in range(1, nz)]
    row_parts = pl.pallas_call(
        functools.partial(forward_kernel, step),
        out_shape=[block] * ncol,
        in_specs=[SMEM] * 4 + [VMEM] * 3,
        out_specs=[VMEM] * ncol,
        scratch_shapes=tables(nrow * stretch) + sums(span),
        compiler_params=params(24),
        cost_estimate=cost,
        name="forward",
    )(pos, rows, cols, counts, tiles, near, far)
    others = [vec_shift(x, t) for t in range(1, nvec) for x in [row_x[0]] + row_x[1:]]
    def by_target(xs):
        return [xs[(ncol - t) % ncol] for t in range(ncol)]

    xs = by_target(row_x)
    for t in range(1, nvec):
        xs += by_target(others[(t - 1) * ncol : t * ncol])
    image, share = pl.pallas_call(
        functools.partial(gram_kernel, nz, ncol, nvec),
        out_shape=[block, jax.ShapeDtypeStruct((nvec, vlocal, vlocal), F32)],
        in_specs=[VMEM] * (nz + ncol + nvec * ncol),
        out_specs=[VMEM] * 2,
        compiler_params=params(8),
        name="gram",
    )(*col_parts, *row_parts, *xs)
    for t in range(1, ncol):
        image = image + col_shift(row_parts[t], t)
    share = all_sum(share, nz, ncol)
    order = lax.rem(k + nvec - jnp.arange(nvec), nvec)
    gram = jnp.take(share, order, axis=0).reshape(nvec * vlocal, vlocal)
    gram = gram / math.sqrt(width * nrow * ncol)
    return (image.astype(jnp.bfloat16), gram)


def all_sum(share, nz, ncol):
    if nz * ncol > 8:
        return lax.psum(share, ("row", "col"))
    nrow = 2 * nz
    share = share + lax.ppermute(share, "row", [(a, a ^ 1) for a in range(nrow)])
    shifts = [(s, t) for s in range(nz) for t in range(ncol) if (s, t) != (0, 0)]
    got = None
    core = lax.axis_index("row") % 2
    for n in range(0, len(shifts), 2):
        pair = shifts[n : n + 2]
        perm = []
        for a in range(nrow):
            for b in range(ncol):
                s, t = pair[(a % 2) % len(pair)]
                perm.append((a * ncol + b, (a + 2 * s) % nrow * ncol + (b + t) % ncol))
        part = lax.ppermute(share, ("row", "col"), perm)
        if len(pair) == 1:
            part = jnp.where(core == 0, part, 0.0)
        got = part if got is None else got + part
    if got is None:
        return share
    return share + got + lax.ppermute(got, "row", [(a, a ^ 1) for a in range(nrow)])


def solution(mesh):
    assert mesh.shape["row"] % 2 == 0
    sizes = (mesh.shape["row"] // 2, mesh.shape["col"], mesh.shape["vec"])
    return jax.shard_map(
        functools.partial(shards, sizes),
        mesh=mesh,
        in_specs=(
            P("vec", ("row", "col")),
            P("row", "col", None, None, None),
            P("row", "col", None),
            P("row", "col", None),
            P("row", "col"),
        ),
        out_specs=(P("vec", ("row", "col")), P(None, "vec")),
        check_vma=False,
    )
```

```python
import functools
import math

import jax
import jax.numpy as jnp
from jax import lax
from jax.experimental import pallas as pl
from jax.experimental.pallas import tpu as pltpu
from jax.sharding import PartitionSpec as P

CHUNK = 32
AHEAD = 2
GROUP = 8
SMEM = pl.BlockSpec(memory_space=pltpu.SMEM)
VMEM = pl.BlockSpec(memory_space=pltpu.VMEM)
HBM = pl.BlockSpec(memory_space=pltpu.HBM)
F32 = jnp.float32
HIGHEST = lax.Precision.HIGHEST


def params(mib):
    return pltpu.CompilerParams(vmem_limit_bytes=mib * 2**20)


def place_block(low, high, block, first, stretch, tile):
    vlocal = block.shape[0]
    zero = jnp.zeros((vlocal, tile), block.dtype)
    for q in range(stretch):
        part = block[:, q * tile : (q + 1) * tile]
        low[first + q] = jnp.concatenate([part, zero], axis=0)
        high[first + q] = jnp.concatenate([zero, part], axis=0)


def multiply_tiles(pick, forward, count, tiles, low, high, sums, arrive=None):
    slots = tiles.shape[0]
    tile = tiles.shape[-1]
    vlocal = sums[0].shape[1]
    for acc in sums:
        acc[...] = jnp.zeros_like(acc)

    def chunk(step, carry):
        if arrive is not None:
            arrive(step)
        for g in range(CHUNK // (2 * GROUP)):
            results = []
            for u in range(GROUP):
                s = step * CHUNK + g * 2 * GROUP + 2 * u
                in0, out0 = pick(s)
                in1, out1 = pick(s + 1)
                left = jnp.concatenate([low[in0], high[in1]], axis=1)
                if forward:
                    right = jnp.concatenate([tiles[s], tiles[s + 1]], axis=1)
                    dims = (((1,), (1,)), ((), ()))
                else:
                    right = tiles[pl.ds(s, 2)].reshape(2 * tile, tile)
                    dims = (((1,), (0,)), ((), ()))
                both = lax.dot_general(left, right, dims, preferred_element_type=F32)
                results.append((both, out0, out1))
            for u, (both, out0, out1) in enumerate(results):
                a, b = sums[(2 * u) % len(sums)], sums[(2 * u + 1) % len(sums)]
                a[out0] += both[:vlocal]
                b[out1] += both[vlocal:]
        return carry

    assert slots % CHUNK == 0
    lax.fori_loop(0, pl.cdiv(count, CHUNK), chunk, 0)


def places(rows, cols, span, stretch):
    def get(s):
        r, c = rows[s], cols[s]
        return r, c, lax.rem(r, span), lax.div(c, span) * stretch + lax.rem(c, stretch)

    return get


def position():
    i = lax.axis_index("row")
    return lax.div(i, 2), lax.rem(i, 2), lax.axis_index("col")


def start_lists(lists, held, sems):
    copies = [pltpu.make_async_copy(a, b, sems.at[n]) for n, (a, b) in enumerate(zip(lists, held))]
    for copy in copies:
        copy.start()
    return copies


def mirror_kernel(sizes, counts, rows_hbm, cols_hbm, tiles_hbm, *refs):
    nz, ncol, stretch = sizes
    span = ncol * stretch
    blocks, (mine, other, tiles), refs = refs[:ncol], refs[ncol : ncol + 3], refs[ncol + 3 :]
    rows, cols, list_sems, tile_sems, low, high, *sums = refs
    slots = tiles.shape[0]
    tile = tiles.shape[-1]
    width = stretch * tile
    copies = start_lists((rows_hbm, cols_hbm), (rows, cols), list_sems)
    count = counts[0]
    chunks = pl.cdiv(count, CHUNK)

    def load(step):
        at = pl.ds(step * CHUNK, CHUNK)
        return pltpu.make_async_copy(tiles_hbm.at[at], tiles.at[at], tile_sems.at[step])

    def start(step):
        @pl.when(step < chunks)
        def _():
            load(step).start()

    for step in range(AHEAD):
        start(step)
    z, core, j = position()
    for t in range(ncol):
        place_block(low, high, blocks[t], lax.rem(j + ncol - t, ncol) * stretch, stretch, tile)
    low[span] = jnp.zeros(low.shape[1:], low.dtype)
    high[span] = jnp.zeros(high.shape[1:], high.dtype)
    get = places(rows, cols, span, stretch)

    def pick(s):
        r, c, row_place, col_place = get(s)
        return jnp.where((s < count) & (r != c), row_place, span), col_place

    def arrive(step):
        load(step).wait()
        start(step + AHEAD)

    for copy in copies:
        copy.wait()
    multiply_tiles(pick, False, count, tiles, low, high, sums, arrive)
    for s in range(nz):
        target = 2 * lax.rem(z + s, nz)
        for out, c in ((mine, core), (other, 1 - core)):
            for q in range(stretch):
                at = (target + c) * stretch + q
                total = sums[0][at]
                for acc in sums[1:]:
                    total += acc[at]
                out[:, s * width + q * tile : s * width + (q + 1) * tile] = total


def forward_kernel(sizes, counts, rows_hbm, cols_hbm, tiles, near, far, *refs):
    nz, ncol, stretch = sizes
    span = ncol * stretch
    outs, (rows, cols, list_sems, low, high, *sums) = refs[:ncol], refs[ncol:]
    tile = tiles.shape[-1]
    width = stretch * tile
    copies = start_lists((rows_hbm, cols_hbm), (rows, cols), list_sems)
    count = counts[0]
    z, core, j = position()
    for s in range(nz):
        source = 2 * lax.rem(z + nz - s, nz)
        for ref, c in ((near, core), (far, 1 - core)):
            place_block(low, high, ref[:, s * width : (s + 1) * width], (source + c) * stretch, stretch, tile)
    dead = 2 * nz * stretch
    low[dead] = jnp.zeros(low.shape[1:], low.dtype)
    high[dead] = jnp.zeros(high.shape[1:], high.dtype)
    get = places(rows, cols, span, stretch)

    def pick(s):
        _, _, row_place, col_place = get(s)
        return jnp.where(s < count, col_place, dead), row_place

    for copy in copies:
        copy.wait()
    multiply_tiles(pick, True, count, tiles, low, high, sums)
    for t in range(ncol):
        first = lax.rem(j + t, ncol) * stretch
        for q in range(stretch):
            total = sums[0][first + q]
            for acc in sums[1:]:
                total += acc[first + q]
            outs[t][:, q * tile : (q + 1) * tile] = total


def pair_kernel(nz, mine, theirs, *outs):
    width = mine.shape[1] // nz
    for s in range(nz):
        at = slice(s * width, (s + 1) * width)
        outs[s][...] = mine[:, at] + theirs[:, at]


def gram_kernel(nz, ncol, nvec, scale, *refs):
    cols, refs = refs[:nz], refs[nz:]
    parts, refs = refs[:ncol], refs[ncol:]
    xs, (image, share) = refs[: nvec * ncol], refs[nvec * ncol :]
    total = parts[0][...]
    for ref in cols:
        total += ref[...]
    image[...] = total
    terms = [total] + [ref[...] for ref in parts[1:]]
    for k in range(nvec):
        product = None
        for t in range(ncol):
            one = lax.dot_general(
                xs[k * ncol + t][...].astype(F32),
                terms[t],
                (((1,), (1,)), ((), ())),
                precision=HIGHEST,
                preferred_element_type=F32,
            )
            product = one if product is None else product + one
        share[lax.rem(lax.axis_index("vec") + nvec - k, nvec)] = product * scale


def shards(sizes, vectors, tile_vals, tile_rows, tile_cols, tile_counts):
    nz, ncol, nvec = sizes
    nrow = 2 * nz
    vlocal, width = vectors.shape
    slots, tile = tile_vals.shape[2], tile_vals.shape[-1]
    stretch = width // tile
    span = ncol * stretch
    tiles, rows, cols, counts = tile_vals[0, 0], tile_rows[0, 0], tile_cols[0, 0], tile_counts[0]

    def core_swap(x):
        return lax.ppermute(x, "row", [(a, a ^ 1) for a in range(nrow)])

    def z_shift(x, s):
        return lax.ppermute(x, "row", [(a, (a + 2 * s) % nrow) for a in range(nrow)])

    def col_shift(x, t):
        return lax.ppermute(x, "col", [(a, (a + t) % ncol) for a in range(ncol)])

    def vec_shift(x, t):
        return lax.ppermute(x, "vec", [(a, (a + t) % nvec) for a in range(nvec)])

    row_x = [vectors] + [col_shift(vectors, t) for t in range(1, ncol)]
    near = jnp.concatenate([vectors] + [z_shift(vectors, s) for s in range(1, nz)], axis=1)
    far = core_swap(near)

    def tables(count):
        shape = pltpu.VMEM((count + 1, 2 * vlocal, tile), vectors.dtype)
        return [shape, shape]

    def sums(count):
        return [pltpu.VMEM((count, vlocal, tile), F32)] * 2

    block = jax.ShapeDtypeStruct((vlocal, width), F32)
    ring = jax.ShapeDtypeStruct((vlocal, nz * width), F32)
    step = (nz, ncol, stretch)
    cost = pl.CostEstimate(
        flops=2 * slots * tile * tile * 2 * vlocal, bytes_accessed=slots * tile * tile * 2, transcendentals=0
    )
    lists = [pltpu.SMEM((slots,), jnp.int32)] * 2 + [pltpu.SemaphoreType.DMA((2,))]
    mine, other, held = pl.pallas_call(
        functools.partial(mirror_kernel, step),
        out_shape=[ring, ring, jax.ShapeDtypeStruct(tiles.shape, tiles.dtype)],
        in_specs=[SMEM] + [HBM] * 3 + [VMEM] * ncol,
        out_specs=[VMEM] * 3,
        scratch_shapes=lists
        + [pltpu.SemaphoreType.DMA((slots // CHUNK,))]
        + tables(span)
        + sums(nrow * stretch),
        compiler_params=params(24),
        cost_estimate=cost,
        name="mirror",
    )(counts, rows, cols, tiles, *row_x)
    theirs = core_swap(other)
    pieces = pl.pallas_call(
        functools.partial(pair_kernel, nz),
        out_shape=[block] * nz,
        in_specs=[VMEM] * 2,
        out_specs=[VMEM] * nz,
        compiler_params=params(8),
        name="pair",
    )(mine, theirs)
    col_parts = [pieces[0]] + [z_shift(pieces[s], s) for s in range(1, nz)]
    row_parts = pl.pallas_call(
        functools.partial(forward_kernel, step),
        out_shape=[block] * ncol,
        in_specs=[SMEM] + [HBM] * 2 + [VMEM] * 3,
        out_specs=[VMEM] * ncol,
        scratch_shapes=lists + tables(nrow * stretch) + sums(span),
        compiler_params=params(24),
        cost_estimate=cost,
        name="forward",
    )(counts, rows, cols, held, near, far)
    others = [vec_shift(x, t) for t in range(1, nvec) for x in [row_x[0]] + row_x[1:]]
    def by_target(xs):
        return [xs[(ncol - t) % ncol] for t in range(ncol)]

    xs = by_target(row_x)
    for t in range(1, nvec):
        xs += by_target(others[(t - 1) * ncol : t * ncol])
    image, share = pl.pallas_call(
        functools.partial(gram_kernel, nz, ncol, nvec, 1.0 / math.sqrt(width * nrow * ncol)),
        out_shape=[block, jax.ShapeDtypeStruct((nvec, vlocal, vlocal), F32)],
        in_specs=[VMEM] * (nz + ncol + nvec * ncol),
        out_specs=[VMEM] * 2,
        compiler_params=params(8),
        name="gram",
    )(*col_parts, *row_parts, *xs)
    for t in range(1, ncol):
        image = image + col_shift(row_parts[t], t)
    share = all_sum(share, nz, ncol)
    gram = share.reshape(nvec * vlocal, vlocal)
    return (image.astype(jnp.bfloat16), gram)


def all_sum(share, nz, ncol):
    if nz * ncol > 8 or nz & (nz - 1):
        return lax.psum(share, ("row", "col"))
    nrow = 2 * nz
    share = share + lax.ppermute(share, "row", [(a, a ^ 1) for a in range(nrow)])
    shifts = sorted(((s, t) for s in range(nz) for t in range(ncol)), key=sum)[1:]
    got = None
    core = lax.axis_index("row") % 2
    for n in range(0, len(shifts), 2):
        pair = shifts[n : n + 2]
        perm = []
        for a in range(nrow):
            for b in range(ncol):
                s, t = pair[(a % 2) % len(pair)]
                perm.append((a * ncol + b, (a ^ (2 * s)) * ncol + (b + t) % ncol))
        part = lax.ppermute(share, ("row", "col"), perm)
        if len(pair) == 1:
            part = jnp.where(core == 0, part, 0.0)
        got = part if got is None else got + part
    if got is None:
        return share
    return share + got + lax.ppermute(got, "row", [(a, a ^ 1) for a in range(nrow)])


def solution(mesh):
    assert mesh.shape["row"] % 2 == 0
    sizes = (mesh.shape["row"] // 2, mesh.shape["col"], mesh.shape["vec"])
    return jax.shard_map(
        functools.partial(shards, sizes),
        mesh=mesh,
        in_specs=(
            P("vec", ("row", "col")),
            P("row", "col", None, None, None),
            P("row", "col", None),
            P("row", "col", None),
            P("row", "col"),
        ),
        out_specs=(P("vec", ("row", "col")), P(None, "vec")),
        check_vma=False,
    )
```

```python
import functools
import math

import jax
import jax.numpy as jnp
from jax import lax
from jax.experimental import pallas as pl
from jax.experimental.pallas import tpu as pltpu
from jax.sharding import PartitionSpec as P

CHUNK = 32
AHEAD = 2
GROUP = 8
SMEM = pl.BlockSpec(memory_space=pltpu.SMEM)
VMEM = pl.BlockSpec(memory_space=pltpu.VMEM)
HBM = pl.BlockSpec(memory_space=pltpu.HBM)
F32 = jnp.float32
HIGHEST = lax.Precision.HIGHEST


def params(mib):
    return pltpu.CompilerParams(vmem_limit_bytes=mib * 2**20)


def place_block(low, high, block, first, stretch, tile):
    vlocal = block.shape[0]
    zero = jnp.zeros((vlocal, tile), block.dtype)
    for q in range(stretch):
        part = block[:, q * tile : (q + 1) * tile]
        low[first + q] = jnp.concatenate([part, zero], axis=0)
        high[first + q] = jnp.concatenate([zero, part], axis=0)


def multiply_tiles(pick, forward, count, tiles, low, high, sums, arrive=None):
    slots = tiles.shape[0]
    tile = tiles.shape[-1]
    vlocal = sums[0].shape[1]
    for acc in sums:
        acc[...] = jnp.zeros_like(acc)

    def chunk(step, carry):
        if arrive is not None:
            arrive(step)
        for g in range(CHUNK // (2 * GROUP)):
            results = []
            for u in range(GROUP):
                s = step * CHUNK + g * 2 * GROUP + 2 * u
                in0, out0 = pick(s)
                in1, out1 = pick(s + 1)
                left = jnp.concatenate([low[in0], high[in1]], axis=1)
                if forward:
                    right = jnp.concatenate([tiles[s], tiles[s + 1]], axis=1)
                    dims = (((1,), (1,)), ((), ()))
                else:
                    right = tiles[pl.ds(s, 2)].reshape(2 * tile, tile)
                    dims = (((1,), (0,)), ((), ()))
                both = lax.dot_general(left, right, dims, preferred_element_type=F32)
                results.append((both, out0, out1))
            for u, (both, out0, out1) in enumerate(results):
                a, b = sums[(2 * u) % len(sums)], sums[(2 * u + 1) % len(sums)]
                a[out0] += both[:vlocal]
                b[out1] += both[vlocal:]
        return carry

    assert slots % CHUNK == 0
    lax.fori_loop(0, pl.cdiv(count, CHUNK), chunk, 0)


def places(rows, cols, span, stretch):
    def get(s):
        r, c = rows[0, s], cols[0, s]
        return r, c, lax.rem(r, span), lax.div(c, span) * stretch + lax.rem(c, stretch)

    return get


def position():
    i = lax.axis_index("row")
    return lax.div(i, 2), lax.rem(i, 2), lax.axis_index("col")


def start_copies(sems, *pairs):
    copies = [pltpu.make_async_copy(a, b, sems.at[n]) for n, (a, b) in enumerate(pairs)]
    for copy in copies:
        copy.start()
    return copies


def mirror_kernel(sizes, counts, rows_hbm, cols_hbm, tiles_hbm, x_hbm, *refs):
    nz, ncol, stretch = sizes
    span = ncol * stretch
    blocks, (mine, other, tiles, x), refs = refs[: ncol - 1], refs[ncol - 1 : ncol + 3], refs[ncol + 3 :]
    rows, cols, small, sems, low, high, *sums = refs
    tile = tiles.shape[-1]
    width = stretch * tile
    count = counts[0, 0]
    chunks = pl.cdiv(count, CHUNK)

    def load(step):
        at = pl.ds(step * CHUNK, CHUNK)
        return pltpu.make_async_copy(tiles_hbm.at[at], tiles.at[at], sems.at[step])

    def start(step):
        @pl.when(step < chunks)
        def _():
            load(step).start()

    copies = start_copies(small, (x_hbm, x), (rows_hbm, rows), (cols_hbm, cols))
    for step in range(AHEAD):
        start(step)
    z, core, j = position()
    for t in range(1, ncol):
        place_block(low, high, blocks[t - 1], lax.rem(j + ncol - t, ncol) * stretch, stretch, tile)
    for copy in copies:
        copy.wait()
    place_block(low, high, x, j * stretch, stretch, tile)
    low[span] = jnp.zeros(low.shape[1:], low.dtype)
    high[span] = jnp.zeros(high.shape[1:], high.dtype)
    get = places(rows, cols, span, stretch)

    def pick(s):
        r, c, row_place, col_place = get(s)
        return jnp.where((s < count) & (r != c), row_place, span), col_place

    def arrive(step):
        load(step).wait()
        start(step + AHEAD)

    multiply_tiles(pick, False, count, tiles, low, high, sums, arrive)
    for s in range(nz):
        target = 2 * lax.rem(z + s, nz)
        for out, c in ((mine, core), (other, 1 - core)):
            for q in range(stretch):
                at = (target + c) * stretch + q
                total = sums[0][at]
                for acc in sums[1:]:
                    total += acc[at]
                out[:, s * width + q * tile : s * width + (q + 1) * tile] = total


def forward_kernel(sizes, counts, rows_hbm, cols_hbm, tiles, near, far, *refs):
    nz, ncol, stretch = sizes
    span = ncol * stretch
    outs, (rows, cols, small, low, high, *sums) = refs[:ncol], refs[ncol:]
    copies = start_copies(small, (rows_hbm, rows), (cols_hbm, cols))
    tile = tiles.shape[-1]
    width = stretch * tile
    count = counts[0, 0]
    z, core, j = position()
    for s in range(nz):
        source = 2 * lax.rem(z + nz - s, nz)
        for ref, c in ((near, core), (far, 1 - core)):
            place_block(low, high, ref[:, s * width : (s + 1) * width], (source + c) * stretch, stretch, tile)
    dead = 2 * nz * stretch
    for copy in copies:
        copy.wait()
    low[dead] = jnp.zeros(low.shape[1:], low.dtype)
    high[dead] = jnp.zeros(high.shape[1:], high.dtype)
    get = places(rows, cols, span, stretch)

    def pick(s):
        _, _, row_place, col_place = get(s)
        return jnp.where(s < count, col_place, dead), row_place

    multiply_tiles(pick, True, count, tiles, low, high, sums)
    for t in range(ncol):
        first = lax.rem(j + t, ncol) * stretch
        for q in range(stretch):
            total = sums[0][first + q]
            for acc in sums[1:]:
                total += acc[first + q]
            outs[t][:, q * tile : (q + 1) * tile] = total


def pair_kernel(nz, mine, theirs, *outs):
    width = mine.shape[1] // nz
    for s in range(nz):
        at = slice(s * width, (s + 1) * width)
        outs[s][...] = mine[:, at] + theirs[:, at]


def gram_kernel(nz, ncol, nvec, scale, *refs):
    cols, refs = refs[:nz], refs[nz:]
    parts, refs = refs[:ncol], refs[ncol:]
    xs, (image, share) = refs[: nvec * ncol], refs[nvec * ncol :]
    total = parts[0][...]
    for ref in cols:
        total += ref[...]
    image[...] = total
    terms = [total] + [ref[...] for ref in parts[1:]]
    products = []
    for k in range(nvec):
        product = None
        for t in range(ncol):
            one = lax.dot_general(
                terms[t],
                xs[k * ncol + t][...].astype(F32),
                (((1,), (1,)), ((), ())),
                precision=HIGHEST,
                preferred_element_type=F32,
            )
            product = one if product is None else product + one
        products.append(product * scale)
    me = lax.axis_index("vec")
    for a in range(nvec):
        picked = products[0]
        for k in range(1, nvec):
            picked = jnp.where(lax.rem(me + nvec - a, nvec) == k, products[k], picked)
        share[:, a * picked.shape[1] : (a + 1) * picked.shape[1]] = picked


def shards(sizes, vectors, tile_vals, tile_rows, tile_cols, tile_counts):
    nz, ncol, nvec = sizes
    nrow = 2 * nz
    vlocal, width = vectors.shape
    slots, tile = tile_vals.shape[2], tile_vals.shape[-1]
    stretch = width // tile
    span = ncol * stretch
    x_hbm, tiles, rows, cols = (
        pltpu.with_memory_space_constraint(a, pltpu.HBM)
        for a in (vectors, tile_vals[0, 0], tile_rows[0], tile_cols[0])
    )

    def core_swap(x):
        return lax.ppermute(x, "row", [(a, a ^ 1) for a in range(nrow)])

    def z_shift(x, s):
        return lax.ppermute(x, "row", [(a, (a + 2 * s) % nrow) for a in range(nrow)])

    def col_shift(x, t):
        return lax.ppermute(x, "col", [(a, (a + t) % ncol) for a in range(ncol)])

    def vec_shift(x, t):
        return lax.ppermute(x, "vec", [(a, (a + t) % nvec) for a in range(nvec)])

    row_x = [vectors] + [col_shift(vectors, t) for t in range(1, ncol)]
    ring_x = [z_shift(vectors, s) for s in range(1, nz)]

    def tables(count):
        shape = pltpu.VMEM((count + 1, 2 * vlocal, tile), vectors.dtype)
        return [shape, shape]

    def sums(count):
        return [pltpu.VMEM((count, vlocal, tile), F32)] * 2

    block = jax.ShapeDtypeStruct((vlocal, width), F32)
    ring = jax.ShapeDtypeStruct((vlocal, nz * width), F32)
    step = (nz, ncol, stretch)
    cost = pl.CostEstimate(
        flops=2 * slots * tile * tile * 2 * vlocal, bytes_accessed=slots * tile * tile * 2, transcendentals=0
    )
    lists = [pltpu.SMEM((1, slots), jnp.int32)] * 2
    mine, other, held, x = pl.pallas_call(
        functools.partial(mirror_kernel, step),
        out_shape=[ring, ring, jax.ShapeDtypeStruct(tiles.shape, tiles.dtype), jax.ShapeDtypeStruct(vectors.shape, vectors.dtype)],
        in_specs=[SMEM] + [HBM] * 4 + [VMEM] * (ncol - 1),
        out_specs=[VMEM] * 4,
        scratch_shapes=lists
        + [pltpu.SemaphoreType.DMA((3,)), pltpu.SemaphoreType.DMA((slots // CHUNK,))]
        + tables(span)
        + sums(nrow * stretch),
        compiler_params=params(6),
        cost_estimate=cost,
        name="mirror",
    )(tile_counts, rows, cols, tiles, x_hbm, *row_x[1:])
    near = jnp.concatenate([x] + ring_x, axis=1)
    far = core_swap(near)
    theirs = core_swap(other)
    pieces = pl.pallas_call(
        functools.partial(pair_kernel, nz),
        out_shape=[block] * nz,
        in_specs=[VMEM] * 2,
        out_specs=[VMEM] * nz,
        compiler_params=params(6),
        name="pair",
    )(mine, theirs)
    col_parts = [pieces[0]] + [z_shift(pieces[s], s) for s in range(1, nz)]
    row_parts = pl.pallas_call(
        functools.partial(forward_kernel, step),
        out_shape=[block] * ncol,
        in_specs=[SMEM] + [HBM] * 2 + [VMEM] * 3,
        out_specs=[VMEM] * ncol,
        scratch_shapes=lists + [pltpu.SemaphoreType.DMA((2,))] + tables(nrow * stretch) + sums(span),
        compiler_params=params(6),
        cost_estimate=cost,
        name="forward",
    )(tile_counts, rows, cols, held, near, far)
    others = [vec_shift(x, t) for t in range(1, nvec) for x in [row_x[0]] + row_x[1:]]
    def by_target(xs):
        return [xs[(ncol - t) % ncol] for t in range(ncol)]

    xs = by_target([x] + row_x[1:])
    for t in range(1, nvec):
        xs += by_target(others[(t - 1) * ncol : t * ncol])
    image, share = pl.pallas_call(
        functools.partial(gram_kernel, nz, ncol, nvec, 1.0 / math.sqrt(width * nrow * ncol)),
        out_shape=[block, jax.ShapeDtypeStruct((vlocal, nvec * vlocal), F32)],
        in_specs=[VMEM] * (nz + ncol + nvec * ncol),
        out_specs=[VMEM] * 2,
        compiler_params=params(6),
        name="gram",
    )(*col_parts, *row_parts, *xs)
    for t in range(1, ncol):
        image = image + col_shift(row_parts[t], t)
    share = all_sum(share, nz, ncol)
    gram = share.T
    return (image.astype(jnp.bfloat16), gram)


def all_sum(share, nz, ncol):
    if nz * ncol > 8 or nz & (nz - 1):
        return lax.psum(share, ("row", "col"))
    nrow = 2 * nz
    share = share + lax.ppermute(share, "row", [(a, a ^ 1) for a in range(nrow)])
    shifts = sorted(((s, t) for s in range(nz) for t in range(ncol)), key=sum)[1:]
    got = None
    for n in range(0, len(shifts), 2):
        pair = shifts[n : n + 2]
        perm = []
        for a in range(nrow):
            for b in range(ncol):
                s, t = pair[(a % 2) % len(pair)]
                perm.append((a * ncol + b, (a ^ (2 * s)) * ncol + (b + t) % ncol))
        part = lax.ppermute(share, ("row", "col"), perm)
        if len(pair) == 1:
            part = part * 0.5
        got = part if got is None else got + part
    if got is None:
        return share
    return share + got + lax.ppermute(got, "row", [(a, a ^ 1) for a in range(nrow)])


def solution(mesh):
    assert mesh.shape["row"] % 2 == 0
    sizes = (mesh.shape["row"] // 2, mesh.shape["col"], mesh.shape["vec"])
    return jax.shard_map(
        functools.partial(shards, sizes),
        mesh=mesh,
        in_specs=(
            P("vec", ("row", "col")),
            P("row", "col", None, None, None),
            P("row", "col", None),
            P("row", "col", None),
            P("row", "col"),
        ),
        out_specs=(P("vec", ("row", "col")), P(None, "vec")),
        check_vma=False,
    )
```

```python
import functools
import math

import jax
import jax.numpy as jnp
from jax import lax
from jax.experimental import pallas as pl
from jax.experimental.pallas import tpu as pltpu
from jax.sharding import PartitionSpec as P

CHUNK = 32
AHEAD = 4
UNROLL = 128
GROUP = 8
VMEM = pl.BlockSpec(memory_space=pltpu.VMEM)
SMEM = pl.BlockSpec(memory_space=pltpu.SMEM)
HBM = pl.BlockSpec(memory_space=pltpu.HBM)
F32 = jnp.float32
HIGHEST = lax.Precision.HIGHEST


def params(mib):
    return pltpu.CompilerParams(vmem_limit_bytes=mib * 2**20)


def place_block(low, high, block, first, stretch, tile):
    vlocal = block.shape[0]
    zero = jnp.zeros((vlocal, tile), block.dtype)
    for q in range(stretch):
        part = block[:, q * tile : (q + 1) * tile]
        low[first + q] = jnp.concatenate([part, zero], axis=0)
        high[first + q] = jnp.concatenate([zero, part], axis=0)


def multiply_tiles(pick, forward, many, count, tiles, low, high, sums, arrive=None):
    slots = tiles.shape[0]
    tile = tiles.shape[-1]
    vlocal = sums[0].shape[1]
    for acc in sums:
        acc[...] = jnp.zeros_like(acc)

    def chunk(step, carry):
        if arrive is not None:
            arrive(step)
        for g in range(many // (2 * GROUP)):
            results = []
            for u in range(GROUP):
                s = step * many + g * 2 * GROUP + 2 * u
                in0, out0 = pick(s)
                in1, out1 = pick(s + 1)
                left = jnp.concatenate([low[in0], high[in1]], axis=1)
                if forward:
                    right = jnp.concatenate([tiles[s], tiles[s + 1]], axis=1)
                    dims = (((1,), (1,)), ((), ()))
                else:
                    right = tiles[pl.ds(s, 2)].reshape(2 * tile, tile)
                    dims = (((1,), (0,)), ((), ()))
                both = lax.dot_general(left, right, dims, preferred_element_type=F32)
                results.append((both, out0, out1))
            for u, (both, out0, out1) in enumerate(results):
                a, b = sums[(2 * u) % len(sums)], sums[(2 * u + 1) % len(sums)]
                a[out0] += both[:vlocal]
                b[out1] += both[vlocal:]
        return carry

    assert slots % many == 0
    lax.fori_loop(0, pl.cdiv(count, many), chunk, 0)


def places(rows, cols, span, stretch):
    def get(s):
        r, c = rows[0, s], cols[0, s]
        return r, c, lax.rem(r, span), lax.div(c, span) * stretch + lax.rem(c, stretch)

    return get


def position():
    i = lax.axis_index("row")
    return lax.div(i, 2), lax.rem(i, 2), lax.axis_index("col")


def start_copies(sems, *pairs):
    copies = [pltpu.make_async_copy(a, b, sems.at[n]) for n, (a, b) in enumerate(pairs)]
    for copy in copies:
        copy.start()
    return copies


def mirror_kernel(sizes, counts, rows_hbm, cols_hbm, tiles_hbm, x_hbm, *refs):
    nz, ncol, stretch = sizes
    span = ncol * stretch
    blocks, (mine, other, tiles, x), refs = refs[: ncol - 1], refs[ncol - 1 : ncol + 3], refs[ncol + 3 :]
    rows, cols, small, sems, low, high, *sums = refs
    tile = tiles.shape[-1]
    width = stretch * tile

    def load(step):
        at = pl.ds(step * CHUNK, CHUNK)
        return pltpu.make_async_copy(tiles_hbm.at[at], tiles.at[at], sems.at[step])

    copies = start_copies(small, (x_hbm, x), (rows_hbm, rows), (cols_hbm, cols))
    ahead = min(AHEAD, tiles.shape[0] // CHUNK)
    for step in range(ahead):
        load(step).start()
    z, core, j = position()
    for t in range(1, ncol):
        place_block(low, high, blocks[t - 1], lax.rem(j + ncol - t, ncol) * stretch, stretch, tile)
    for copy in copies:
        copy.wait()
    count = counts[0, 0]
    chunks = pl.cdiv(count, CHUNK)
    place_block(low, high, x, j * stretch, stretch, tile)
    low[span] = jnp.zeros(low.shape[1:], low.dtype)
    high[span] = jnp.zeros(high.shape[1:], high.dtype)
    get = places(rows, cols, span, stretch)

    def pick(s):
        r, c, row_place, col_place = get(s)
        return jnp.where((s < count) & (r != c), row_place, span), col_place

    def arrive(step):
        load(step).wait()

        @pl.when(step + ahead < chunks)
        def _():
            load(step + ahead).start()

    multiply_tiles(pick, False, CHUNK, count, tiles, low, high, sums, arrive)
    for step in range(1, ahead):

        @pl.when(step >= chunks)
        def _():
            load(step).wait()

    for s in range(nz):
        target = 2 * lax.rem(z + s, nz)
        for out, c in ((mine, core), (other, 1 - core)):
            for q in range(stretch):
                at = (target + c) * stretch + q
                total = sums[0][at]
                for acc in sums[1:]:
                    total += acc[at]
                out[:, s * width + q * tile : s * width + (q + 1) * tile] = total


def forward_kernel(sizes, counts, rows_hbm, cols_hbm, tiles, near, far, *refs):
    nz, ncol, stretch = sizes
    span = ncol * stretch
    outs, (rows, cols, small, low, high, *sums) = refs[:ncol], refs[ncol:]
    copies = start_copies(small, (rows_hbm, rows), (cols_hbm, cols))
    tile = tiles.shape[-1]
    width = stretch * tile
    z, core, j = position()
    for s in range(nz):
        source = 2 * lax.rem(z + nz - s, nz)
        for ref, c in ((near, core), (far, 1 - core)):
            place_block(low, high, ref[:, s * width : (s + 1) * width], (source + c) * stretch, stretch, tile)
    dead = 2 * nz * stretch
    for copy in copies:
        copy.wait()
    count = counts[0, 0]
    low[dead] = jnp.zeros(low.shape[1:], low.dtype)
    high[dead] = jnp.zeros(high.shape[1:], high.dtype)
    get = places(rows, cols, span, stretch)

    def pick(s):
        _, _, row_place, col_place = get(s)
        return jnp.where(s < count, col_place, dead), row_place

    multiply_tiles(pick, True, UNROLL, count, tiles, low, high, sums)
    for t in range(ncol):
        first = lax.rem(j + t, ncol) * stretch
        for q in range(stretch):
            total = sums[0][first + q]
            for acc in sums[1:]:
                total += acc[first + q]
            outs[t][:, q * tile : (q + 1) * tile] = total


def pair_kernel(nz, mine, theirs, *outs):
    width = mine.shape[1] // nz
    for s in range(nz):
        at = slice(s * width, (s + 1) * width)
        outs[s][...] = mine[:, at] + theirs[:, at]


def gram_kernel(nz, ncol, nvec, scale, *refs):
    cols, refs = refs[:nz], refs[nz:]
    parts, refs = refs[:ncol], refs[ncol:]
    xs, (image, share) = refs[: nvec * ncol], refs[nvec * ncol :]
    total = parts[0][...]
    for ref in cols:
        total += ref[...]
    image[...] = total
    terms = [total] + [ref[...] for ref in parts[1:]]
    products = []
    for k in range(nvec):
        product = None
        for t in range(ncol):
            one = lax.dot_general(
                terms[t],
                xs[k * ncol + t][...].astype(F32),
                (((1,), (1,)), ((), ())),
                precision=HIGHEST,
                preferred_element_type=F32,
            )
            product = one if product is None else product + one
        products.append(product * scale)
    me = lax.axis_index("vec")
    for a in range(nvec):
        picked = products[0]
        for k in range(1, nvec):
            picked = jnp.where(lax.rem(me + nvec - a, nvec) == k, products[k], picked)
        share[:, a * picked.shape[1] : (a + 1) * picked.shape[1]] = picked


def shards(sizes, vectors, tile_vals, tile_rows, tile_cols, tile_counts):
    nz, ncol, nvec = sizes
    nrow = 2 * nz
    vlocal, width = vectors.shape
    slots, tile = tile_vals.shape[2], tile_vals.shape[-1]
    stretch = width // tile
    span = ncol * stretch
    x_hbm, tiles, rows, cols = (
        pltpu.with_memory_space_constraint(a, pltpu.HBM)
        for a in (vectors, tile_vals[0, 0], tile_rows[0], tile_cols[0])
    )

    def core_swap(x):
        return lax.ppermute(x, "row", [(a, a ^ 1) for a in range(nrow)])

    def z_shift(x, s):
        return lax.ppermute(x, "row", [(a, (a + 2 * s) % nrow) for a in range(nrow)])

    def col_shift(x, t):
        return lax.ppermute(x, "col", [(a, (a + t) % ncol) for a in range(ncol)])

    def vec_shift(x, t):
        return lax.ppermute(x, "vec", [(a, (a + t) % nvec) for a in range(nvec)])

    row_x = [vectors] + [col_shift(vectors, t) for t in range(1, ncol)]
    ring_x = [z_shift(vectors, s) for s in range(1, nz)]

    def tables(count):
        shape = pltpu.VMEM((count + 1, 2 * vlocal, tile), vectors.dtype)
        return [shape, shape]

    def sums(count):
        return [pltpu.VMEM((count, vlocal, tile), F32)] * 2

    block = jax.ShapeDtypeStruct((vlocal, width), F32)
    ring = jax.ShapeDtypeStruct((vlocal, nz * width), F32)
    step = (nz, ncol, stretch)
    cost = pl.CostEstimate(
        flops=2 * slots * tile * tile * 2 * vlocal, bytes_accessed=slots * tile * tile * 2, transcendentals=0
    )
    lists = [pltpu.SMEM((1, slots), jnp.int32)] * 2
    mine, other, held, x = pl.pallas_call(
        functools.partial(mirror_kernel, step),
        out_shape=[ring, ring, jax.ShapeDtypeStruct(tiles.shape, tiles.dtype), jax.ShapeDtypeStruct(vectors.shape, vectors.dtype)],
        in_specs=[SMEM] + [HBM] * 4 + [VMEM] * (ncol - 1),
        out_specs=[VMEM] * 4,
        scratch_shapes=lists
        + [pltpu.SemaphoreType.DMA((3,)), pltpu.SemaphoreType.DMA((slots // CHUNK,))]
        + tables(span)
        + sums(nrow * stretch),
        compiler_params=params(6),
        cost_estimate=cost,
        name="mirror",
    )(tile_counts, rows, cols, tiles, x_hbm, *row_x[1:])
    near = jnp.concatenate([x] + ring_x, axis=1)
    far = core_swap(near)
    theirs = core_swap(other)
    pieces = pl.pallas_call(
        functools.partial(pair_kernel, nz),
        out_shape=[block] * nz,
        in_specs=[VMEM] * 2,
        out_specs=[VMEM] * nz,
        compiler_params=params(6),
        name="pair",
    )(mine, theirs)
    col_parts = [pieces[0]] + [z_shift(pieces[s], s) for s in range(1, nz)]
    row_parts = pl.pallas_call(
        functools.partial(forward_kernel, step),
        out_shape=[block] * ncol,
        in_specs=[SMEM] + [HBM] * 2 + [VMEM] * 3,
        out_specs=[VMEM] * ncol,
        scratch_shapes=lists + [pltpu.SemaphoreType.DMA((2,))] + tables(nrow * stretch) + sums(span),
        compiler_params=params(6),
        cost_estimate=cost,
        name="forward",
    )(tile_counts, rows, cols, held, near, far)
    others = [vec_shift(x, t) for t in range(1, nvec) for x in [row_x[0]] + row_x[1:]]
    def by_target(xs):
        return [xs[(ncol - t) % ncol] for t in range(ncol)]

    xs = by_target([x] + row_x[1:])
    for t in range(1, nvec):
        xs += by_target(others[(t - 1) * ncol : t * ncol])
    image, share = pl.pallas_call(
        functools.partial(gram_kernel, nz, ncol, nvec, 1.0 / math.sqrt(width * nrow * ncol)),
        out_shape=[block, jax.ShapeDtypeStruct((vlocal, nvec * vlocal), F32)],
        in_specs=[VMEM] * (nz + ncol + nvec * ncol),
        out_specs=[VMEM] * 2,
        compiler_params=params(6),
        name="gram",
    )(*col_parts, *row_parts, *xs)
    for t in range(1, ncol):
        image = image + col_shift(row_parts[t], t)
    share = all_sum(share, nz, ncol)
    gram = share.T
    return (image.astype(jnp.bfloat16), gram)


def all_sum(share, nz, ncol):
    if nz * ncol > 8 or nz & (nz - 1) or nz == 1:
        return lax.psum(share, ("row", "col"))
    nrow = 2 * nz

    def send(x, pair):
        perm = []
        for a in range(nrow):
            for b in range(ncol):
                s, t = pair[a % 2]
                perm.append((a * ncol + b, (a ^ (2 * s)) * ncol + (b + t) % ncol))
        return lax.ppermute(x, ("row", "col"), perm)

    def swap(x):
        return lax.ppermute(x, "row", [(a, a ^ 1) for a in range(nrow)])

    got = send(share, ((1, 0), (1, 0)))
    share = share + swap(share)
    shifts = [(s, t) for s in range(nz) for t in range(ncol) if (s, t) not in ((0, 0), (1, 0))]
    for n in range(0, len(shifts) - 1, 2):
        got = got + send(share, shifts[n : n + 2])
    if len(shifts) % 2:
        got = got + 0.5 * send(share, shifts[-1:] * 2)
    return share + got + swap(got)


def solution(mesh):
    assert mesh.shape["row"] % 2 == 0
    sizes = (mesh.shape["row"] // 2, mesh.shape["col"], mesh.shape["vec"])
    return jax.shard_map(
        functools.partial(shards, sizes),
        mesh=mesh,
        in_specs=(
            P("vec", ("row", "col")),
            P("row", "col", None, None, None),
            P("row", "col", None),
            P("row", "col", None),
            P("row", "col"),
        ),
        out_specs=(P("vec", ("row", "col")), P(None, "vec")),
        check_vma=False,
    )
```

```python
import functools
import math

import jax
import jax.numpy as jnp
from jax import lax
from jax.experimental import pallas as pl
from jax.experimental.pallas import tpu as pltpu
from jax.sharding import PartitionSpec as P

UNROLL = 128
LONGER = 4
GROUP = 8
VMEM = pl.BlockSpec(memory_space=pltpu.VMEM)
SMEM = pl.BlockSpec(memory_space=pltpu.SMEM)
HBM = pl.BlockSpec(memory_space=pltpu.HBM)
F32 = jnp.float32
HIGHEST = lax.Precision.HIGHEST


def params(mib):
    return pltpu.CompilerParams(vmem_limit_bytes=mib * 2**20)


def place_block(low, high, block, first, stretch, tile):
    vlocal = block.shape[0]
    zero = jnp.zeros((vlocal, tile), block.dtype)
    for q in range(stretch):
        part = block[:, q * tile : (q + 1) * tile]
        low[first + q] = jnp.concatenate([part, zero], axis=0)
        high[first + q] = jnp.concatenate([zero, part], axis=0)


def multiply_tiles(pick, forward, many, count, tiles, low, high, sums):
    slots = tiles.shape[0]
    tile = tiles.shape[-1]
    vlocal = sums[0].shape[1]
    for acc in sums:
        acc[...] = jnp.zeros_like(acc)

    def chunk(step, carry):
        for g in range(many // (2 * GROUP)):
            results = []
            for u in range(GROUP):
                s = step * many + g * 2 * GROUP + 2 * u
                in0, out0 = pick(s)
                in1, out1 = pick(s + 1)
                left = jnp.concatenate([low[in0], high[in1]], axis=1)
                if forward:
                    right = jnp.concatenate([tiles[s], tiles[s + 1]], axis=1)
                    dims = (((1,), (1,)), ((), ()))
                else:
                    right = tiles[pl.ds(s, 2)].reshape(2 * tile, tile)
                    dims = (((1,), (0,)), ((), ()))
                both = lax.dot_general(left, right, dims, preferred_element_type=F32)
                results.append((both, out0, out1))
            for u, (both, out0, out1) in enumerate(results):
                a, b = sums[(2 * u) % len(sums)], sums[(2 * u + 1) % len(sums)]
                a[out0] += both[:vlocal]
                b[out1] += both[vlocal:]
        return carry

    assert slots % many == 0
    lax.fori_loop(0, pl.cdiv(count, many), chunk, 0)


def places(rows, cols, span, stretch):
    def get(s):
        r, c = rows[0, s], cols[0, s]
        return r, c, lax.rem(r, span), lax.div(c, span) * stretch + lax.rem(c, stretch)

    return get


def position():
    i = lax.axis_index("row")
    return lax.div(i, 2), lax.rem(i, 2), lax.axis_index("col")


def start_copies(sems, *pairs):
    copies = [pltpu.make_async_copy(a, b, sems.at[n]) for n, (a, b) in enumerate(pairs)]
    for copy in copies:
        copy.start()
    return copies


def stage_kernel(tiles, token):
    token[...] = jnp.zeros_like(token)


def mirror_kernel(sizes, counts, rows_hbm, cols_hbm, tiles, x_hbm, token, *refs):
    nz, ncol, stretch = sizes
    span = ncol * stretch
    blocks, (mine, other, x, wide), refs = refs[: ncol - 1], refs[ncol - 1 : ncol + 3], refs[ncol + 3 :]
    rows, cols, small, low, high, *sums = refs
    tile = tiles.shape[-1]
    width = stretch * tile

    copies = start_copies(small, (x_hbm, x), (rows_hbm, rows), (cols_hbm, cols))
    z, core, j = position()
    for t in range(1, ncol):
        wide[:, t * width : (t + 1) * width] = blocks[t - 1][...]
        place_block(low, high, blocks[t - 1], lax.rem(j + ncol - t, ncol) * stretch, stretch, tile)
    for copy in copies:
        copy.wait()
    count = counts[0, 0]
    wide[:, :width] = x[...]
    wide[:, ncol * width :] = jnp.zeros_like(wide[:, ncol * width :])
    place_block(low, high, x, j * stretch, stretch, tile)
    low[span] = jnp.zeros(low.shape[1:], low.dtype)
    high[span] = jnp.zeros(high.shape[1:], high.dtype)
    get = places(rows, cols, span, stretch)

    def pick(s):
        r, c, row_place, col_place = get(s)
        return jnp.where((s < count) & (r != c), row_place, span), col_place

    multiply_tiles(pick, False, UNROLL, count, tiles, low, high, sums)
    for s in range(nz):
        target = 2 * lax.rem(z + s, nz)
        for out, c in ((mine, core), (other, 1 - core)):
            for q in range(stretch):
                at = (target + c) * stretch + q
                total = sums[0][at]
                for acc in sums[1:]:
                    total += acc[at]
                out[:, s * width + q * tile : s * width + (q + 1) * tile] = total


def forward_kernel(sizes, counts, rows_hbm, cols_hbm, tiles, near, far, *refs):
    nz, ncol, stretch = sizes
    span = ncol * stretch
    outs, (rows, cols, small, low, high, *sums) = refs[:ncol], refs[ncol:]
    copies = start_copies(small, (rows_hbm, rows), (cols_hbm, cols))
    tile = tiles.shape[-1]
    width = stretch * tile
    z, core, j = position()
    for s in range(nz):
        source = 2 * lax.rem(z + nz - s, nz)
        for ref, c in ((near, core), (far, 1 - core)):
            place_block(low, high, ref[:, s * width : (s + 1) * width], (source + c) * stretch, stretch, tile)
    dead = 2 * nz * stretch
    for copy in copies:
        copy.wait()
    count = counts[0, 0]
    low[dead] = jnp.zeros(low.shape[1:], low.dtype)
    high[dead] = jnp.zeros(high.shape[1:], high.dtype)
    get = places(rows, cols, span, stretch)

    def pick(s):
        _, _, row_place, col_place = get(s)
        return jnp.where(s < count, col_place, dead), row_place

    multiply_tiles(pick, True, UNROLL, count, tiles, low, high, sums)
    for t in range(ncol):
        first = lax.rem(j + t, ncol) * stretch
        for q in range(stretch):
            total = sums[0][first + q]
            for acc in sums[1:]:
                total += acc[first + q]
            outs[t][:, q * tile : (q + 1) * tile] = total


def pair_kernel(nz, mine, theirs, *outs):
    width = mine.shape[1] // nz
    for s in range(nz):
        at = slice(s * width, (s + 1) * width)
        outs[s][...] = mine[:, at] + theirs[:, at]


def gram_kernel(nz, ncol, nvec, scale, *refs):
    cols, refs = refs[:nz], refs[nz:]
    parts, refs = refs[:ncol], refs[ncol:]
    xs, (image, share, *messages) = refs[:nvec], refs[nvec:]
    width = image.shape[1]
    total = parts[0][...]
    for ref in cols:
        total += ref[...]
    image[...] = total
    terms = jnp.concatenate([total] + [parts[ncol - t][...] for t in range(1, ncol)], axis=1)
    products = [
        scale
        * lax.dot_general(
            terms,
            ref[:, : terms.shape[1]].astype(F32),
            (((1,), (1,)), ((), ())),
            precision=HIGHEST,
            preferred_element_type=F32,
        )
        for ref in xs
    ]
    me = lax.axis_index("vec")
    for a in range(nvec):
        picked = products[0]
        for k in range(1, nvec):
            picked = jnp.where(lax.rem(me + nvec - a, nvec) == k, products[k], picked)
        share[:, a * picked.shape[1] : (a + 1) * picked.shape[1]] = picked
    for t in range(1, ncol):
        message = messages[t - 1]
        message[:, :width] = parts[t][...]
        message[:, width:] = jnp.zeros_like(message[:, width:])
        message[:, width : width + share.shape[1]] = share[...]


def shards(sizes, vectors, tile_vals, tile_rows, tile_cols, tile_counts):
    nz, ncol, nvec = sizes
    nrow = 2 * nz
    vlocal, width = vectors.shape
    slots, tile = tile_vals.shape[2], tile_vals.shape[-1]
    stretch = width // tile
    span = ncol * stretch
    x_hbm, tiles_hbm = (
        pltpu.with_memory_space_constraint(a, pltpu.HBM)
        for a in (vectors, tile_vals[0, 0])
    )
    tiles, rows, cols = tile_vals[0, 0], tile_rows[0], tile_cols[0]
    token = pl.pallas_call(
        stage_kernel,
        out_shape=jax.ShapeDtypeStruct((vlocal, tile), F32),
        in_specs=[HBM],
        out_specs=VMEM,
        compiler_params=params(6),
        cost_estimate=pl.CostEstimate(flops=0, bytes_accessed=2 * tile_vals.size * 2, transcendentals=0),
        name="stage",
    )(tiles_hbm)
    vectors, token = lax.optimization_barrier((vectors, token))

    def core_swap(x):
        return lax.ppermute(x, "row", [(a, a ^ 1) for a in range(nrow)])

    def z_shift(x, s):
        return lax.ppermute(x, "row", [(a, (a + 2 * s) % nrow) for a in range(nrow)])

    def col_shift(x, t):
        return lax.ppermute(x, "col", [(a, (a + t) % ncol) for a in range(ncol)])

    def vec_shift(x, t):
        return lax.ppermute(x, "vec", [(a, (a + t) % nvec) for a in range(nvec)])

    row_x = [vectors] + [col_shift(vectors, t) for t in range(1, ncol)]
    ring_x = [z_shift(vectors, s) for s in range(1, nz)]

    def tables(count):
        shape = pltpu.VMEM((count + 1, 2 * vlocal, tile), vectors.dtype)
        return [shape, shape]

    def sums(count):
        return [pltpu.VMEM((count, vlocal, tile), F32)] * 2

    block = jax.ShapeDtypeStruct((vlocal, width), F32)
    ring = jax.ShapeDtypeStruct((vlocal, nz * width), F32)
    step = (nz, ncol, stretch)
    cost = pl.CostEstimate(
        flops=2 * slots * tile * tile * 2 * vlocal, bytes_accessed=slots * tile * tile * 2, transcendentals=0
    )
    lists = [pltpu.SMEM((1, slots), jnp.int32)] * 2
    mine, other, x, wide = pl.pallas_call(
        functools.partial(mirror_kernel, step),
        out_shape=[ring, ring, jax.ShapeDtypeStruct(vectors.shape, vectors.dtype), jax.ShapeDtypeStruct((vlocal, LONGER * ncol * width), vectors.dtype)],
        in_specs=[SMEM] + [VMEM] * 3 + [HBM] + [VMEM] * ncol,
        out_specs=[VMEM] * 4,
        scratch_shapes=lists
        + [pltpu.SemaphoreType.DMA((3,))]
        + tables(span)
        + sums(nrow * stretch),
        compiler_params=params(6),
        cost_estimate=cost,
        name="mirror",
    )(tile_counts, rows, cols, tiles, x_hbm, token, *row_x[1:])
    near = jnp.concatenate([x] + ring_x, axis=1)
    far = core_swap(near)
    theirs = core_swap(other)
    pieces = pl.pallas_call(
        functools.partial(pair_kernel, nz),
        out_shape=[block] * nz,
        in_specs=[VMEM] * 2,
        out_specs=[VMEM] * nz,
        compiler_params=params(6),
        name="pair",
    )(mine, theirs)
    col_parts = [pieces[0]] + [z_shift(pieces[s], s) for s in range(1, nz)]
    row_parts = pl.pallas_call(
        functools.partial(forward_kernel, step),
        out_shape=[block] * ncol,
        in_specs=[SMEM] + [VMEM] * 5,
        out_specs=[VMEM] * ncol,
        scratch_shapes=lists + [pltpu.SemaphoreType.DMA((2,))] + tables(nrow * stretch) + sums(span),
        compiler_params=params(6),
        cost_estimate=cost,
        name="forward",
    )(tile_counts, rows, cols, tiles, near, far)
    every_x = [wide] + [vec_shift(wide, t) for t in range(1, nvec)]
    pad = -(-nvec * vlocal // tile) * tile
    message = jax.ShapeDtypeStruct((vlocal, width + pad), F32)
    image, share, *messages = pl.pallas_call(
        functools.partial(gram_kernel, nz, ncol, nvec, 1.0 / math.sqrt(width * nrow * ncol)),
        out_shape=[block, jax.ShapeDtypeStruct((vlocal, nvec * vlocal), F32)] + [message] * (ncol - 1),
        in_specs=[VMEM] * (nz + ncol + nvec),
        out_specs=[VMEM] * (ncol + 1),
        compiler_params=params(6),
        name="gram",
    )(*col_parts, *row_parts, *every_x)
    got = jnp.zeros_like(share)
    for t in range(1, ncol):
        message = col_shift(messages[t - 1], t)
        image = image + message[:, :width]
        got = got + message[:, width : width + share.shape[1]]
    share = all_sum(share, got, nz, ncol, messages[0])
    gram = share.T
    return (image.astype(jnp.bfloat16), gram)


def all_sum(share, got, nz, ncol, message):
    if nz * ncol > 8 or nz & (nz - 1) or ncol % 2:
        return lax.psum(share, ("row", "col"))
    nrow = 2 * nz

    def send(x, s, t):
        perm = []
        for a in range(nrow):
            for b in range(ncol):
                perm.append((a * ncol + b, (a ^ (2 * s)) * ncol + (b + t + a % 2) % ncol))
        return lax.ppermute(x, ("row", "col"), perm)

    def swap(x):
        return lax.ppermute(x, "row", [(a, a ^ 1) for a in range(nrow)])

    share = share + swap(message)[:, -(-share.shape[1] // 128) * 128 * -1 :][:, : share.shape[1]]
    for s in range(1, nz):
        for t in range(0, ncol, 2):
            got = got + send(share, s, t)
    return share + got + swap(got)


def solution(mesh):
    assert mesh.shape["row"] % 2 == 0
    sizes = (mesh.shape["row"] // 2, mesh.shape["col"], mesh.shape["vec"])
    return jax.shard_map(
        functools.partial(shards, sizes),
        mesh=mesh,
        in_specs=(
            P("vec", ("row", "col")),
            P("row", "col", None, None, None),
            P("row", "col", None),
            P("row", "col", None),
            P("row", "col"),
        ),
        out_specs=(P("vec", ("row", "col")), P(None, "vec")),
        check_vma=False,
    )
```

```python
import functools
import math

import jax
import jax.numpy as jnp
from jax import lax
from jax.experimental import pallas as pl
from jax.experimental.pallas import tpu as pltpu
from jax.sharding import PartitionSpec as P

UNROLL = 128
LONGER = 4
GROUP = 8
VMEM = pl.BlockSpec(memory_space=pltpu.VMEM)
SMEM = pl.BlockSpec(memory_space=pltpu.SMEM)
HBM = pl.BlockSpec(memory_space=pltpu.HBM)
F32 = jnp.float32
HIGHEST = lax.Precision.HIGHEST


def params(mib):
    return pltpu.CompilerParams(vmem_limit_bytes=mib * 2**20)


def place_block(low, high, block, first, stretch, tile):
    vlocal = block.shape[0]
    zero = jnp.zeros((vlocal, tile), block.dtype)
    for q in range(stretch):
        part = block[:, q * tile : (q + 1) * tile]
        low[first + q] = jnp.concatenate([part, zero], axis=0)
        high[first + q] = jnp.concatenate([zero, part], axis=0)


def multiply_tiles(pick, forward, many, count, tiles, low, high, sums):
    slots = tiles.shape[0]
    tile = tiles.shape[-1]
    vlocal = sums[0].shape[1]
    for acc in sums:
        acc[...] = jnp.zeros_like(acc)

    def chunk(step, carry):
        for g in range(many // (2 * GROUP)):
            results = []
            for u in range(GROUP):
                s = step * many + g * 2 * GROUP + 2 * u
                in0, out0 = pick(s)
                in1, out1 = pick(s + 1)
                left = jnp.concatenate([low[in0], high[in1]], axis=1)
                if forward:
                    right = jnp.concatenate([tiles[s], tiles[s + 1]], axis=1)
                    dims = (((1,), (1,)), ((), ()))
                else:
                    right = tiles[pl.ds(s, 2)].reshape(2 * tile, tile)
                    dims = (((1,), (0,)), ((), ()))
                both = lax.dot_general(left, right, dims, preferred_element_type=F32)
                results.append((both, out0, out1))
            for u, (both, out0, out1) in enumerate(results):
                a, b = sums[(2 * u) % len(sums)], sums[(2 * u + 1) % len(sums)]
                a[out0] += both[:vlocal]
                b[out1] += both[vlocal:]
        return carry

    assert slots % many == 0
    lax.fori_loop(0, pl.cdiv(count, many), chunk, 0)


def divide(x, n):
    if n & (n - 1):
        return lax.div(x, n), lax.rem(x, n)
    return x >> (n.bit_length() - 1), x & (n - 1)


def places(rows, cols, span, stretch):
    group, inner = divide(cols[...], span)
    return divide(rows[...], span)[1], group * stretch + divide(inner, stretch)[1]


def hand_scalars(held, sem, *lists):
    vector, scalar = held
    for n, values in enumerate(lists):
        vector[n : n + 1, :] = values
    copy = pltpu.make_async_copy(vector, scalar, sem)
    copy.start()
    return copy


def position():
    i = lax.axis_index("row")
    return lax.div(i, 2), lax.rem(i, 2), lax.axis_index("col")


def stage_kernel(tiles, token):
    token[...] = jnp.zeros_like(token)


def mirror_kernel(sizes, counts, rows, cols, tiles, x_hbm, token, *refs):
    nz, ncol, stretch = sizes
    span = ncol * stretch
    blocks, (mine, other, x, wide), refs = refs[: ncol - 1], refs[ncol - 1 : ncol + 3], refs[ncol + 3 :]
    vector, scalar, sems, low, high, *sums = refs
    tile = tiles.shape[-1]
    width = stretch * tile
    count = counts[0, 0]
    own = pltpu.make_async_copy(x_hbm, x, sems.at[0])
    own.start()
    slot = lax.broadcasted_iota(jnp.int32, rows.shape, 1)
    row_place, col_place = places(rows, cols, span, stretch)
    used = jnp.where((slot < count) & (rows[...] != cols[...]), row_place, span)
    indices = hand_scalars((vector, scalar), sems.at[1], used, col_place)
    z, core, j = position()
    for t in range(1, ncol):
        wide[:, t * width : (t + 1) * width] = blocks[t - 1][...]
        place_block(low, high, blocks[t - 1], lax.rem(j + ncol - t, ncol) * stretch, stretch, tile)
    own.wait()
    wide[:, :width] = x[...]
    wide[:, ncol * width :] = jnp.zeros_like(wide[:, ncol * width :])
    place_block(low, high, x, j * stretch, stretch, tile)
    low[span] = jnp.zeros(low.shape[1:], low.dtype)
    high[span] = jnp.zeros(high.shape[1:], high.dtype)
    indices.wait()

    def pick(s):
        return scalar[0, s], scalar[1, s]

    multiply_tiles(pick, False, UNROLL, count, tiles, low, high, sums)
    for s in range(nz):
        target = 2 * lax.rem(z + s, nz)
        for out, c in ((mine, core), (other, 1 - core)):
            for q in range(stretch):
                at = (target + c) * stretch + q
                total = sums[0][at]
                for acc in sums[1:]:
                    total += acc[at]
                out[:, s * width + q * tile : s * width + (q + 1) * tile] = total


def forward_kernel(sizes, counts, rows, cols, tiles, near, far, *refs):
    nz, ncol, stretch = sizes
    span = ncol * stretch
    outs, (vector, scalar, sem, low, high, *sums) = refs[:ncol], refs[ncol:]
    dead = 2 * nz * stretch
    slot = lax.broadcasted_iota(jnp.int32, rows.shape, 1)
    row_place, col_place = places(rows, cols, span, stretch)
    indices = hand_scalars((vector, scalar), sem, jnp.where(slot < counts[0, 0], col_place, dead), row_place)
    tile = tiles.shape[-1]
    width = stretch * tile
    z, core, j = position()
    for s in range(nz):
        source = 2 * lax.rem(z + nz - s, nz)
        for ref, c in ((near, core), (far, 1 - core)):
            place_block(low, high, ref[:, s * width : (s + 1) * width], (source + c) * stretch, stretch, tile)
    low[dead] = jnp.zeros(low.shape[1:], low.dtype)
    high[dead] = jnp.zeros(high.shape[1:], high.dtype)
    indices.wait()

    def pick(s):
        return scalar[0, s], scalar[1, s]

    multiply_tiles(pick, True, UNROLL, counts[0, 0], tiles, low, high, sums)
    for t in range(ncol):
        first = lax.rem(j + t, ncol) * stretch
        for q in range(stretch):
            total = sums[0][first + q]
            for acc in sums[1:]:
                total += acc[first + q]
            outs[t][:, q * tile : (q + 1) * tile] = total


def pair_kernel(nz, mine, theirs, *outs):
    width = mine.shape[1] // nz
    for s in range(nz):
        at = slice(s * width, (s + 1) * width)
        outs[s][...] = mine[:, at] + theirs[:, at]


def gram_kernel(nz, ncol, nvec, scale, *refs):
    cols, refs = refs[:nz], refs[nz:]
    parts, refs = refs[:ncol], refs[ncol:]
    xs, (image, share, *messages) = refs[:nvec], refs[nvec:]
    width = image.shape[1]
    total = parts[0][...]
    for ref in cols:
        total += ref[...]
    image[...] = total
    terms = jnp.concatenate([total] + [parts[ncol - t][...] for t in range(1, ncol)], axis=1)
    split = []
    rest = terms
    for _ in range(3):
        part = rest.astype(jnp.bfloat16)
        split.append(part)
        rest = rest - part.astype(F32)
    split = jnp.concatenate(split, axis=0)
    vlocal = terms.shape[0]
    every = jnp.concatenate([ref[:, : terms.shape[1]] for ref in xs], axis=0)
    thirds = lax.dot_general(split, every, (((1,), (1,)), ((), ())), preferred_element_type=F32)
    whole = scale * (thirds[:vlocal] + thirds[vlocal : 2 * vlocal] + thirds[2 * vlocal :])
    products = [whole[:, k * vlocal : (k + 1) * vlocal] for k in range(nvec)]
    me = lax.axis_index("vec")
    for a in range(nvec):
        picked = products[0]
        for k in range(1, nvec):
            picked = jnp.where(lax.rem(me + nvec - a, nvec) == k, products[k], picked)
        share[:, a * picked.shape[1] : (a + 1) * picked.shape[1]] = picked
    for t in range(1, ncol):
        message = messages[t - 1]
        message[:, :width] = parts[t][...]
        message[:, width:] = jnp.zeros_like(message[:, width:])
        message[:, width : width + share.shape[1]] = share[...]


def shards(sizes, vectors, tile_vals, tile_rows, tile_cols, tile_counts):
    nz, ncol, nvec = sizes
    nrow = 2 * nz
    vlocal, width = vectors.shape
    slots, tile = tile_vals.shape[2], tile_vals.shape[-1]
    stretch = width // tile
    span = ncol * stretch
    x_hbm, tiles_hbm = (
        pltpu.with_memory_space_constraint(a, pltpu.HBM)
        for a in (vectors, tile_vals[0, 0])
    )
    tiles, rows, cols = tile_vals[0, 0], tile_rows[0], tile_cols[0]
    token = pl.pallas_call(
        stage_kernel,
        out_shape=jax.ShapeDtypeStruct((vlocal, tile), F32),
        in_specs=[HBM],
        out_specs=VMEM,
        compiler_params=params(6),
        cost_estimate=pl.CostEstimate(flops=0, bytes_accessed=2 * tile_vals.size * 2, transcendentals=0),
        name="stage",
    )(tiles_hbm)
    vectors, token = lax.optimization_barrier((vectors, token))

    def core_swap(x):
        return lax.ppermute(x, "row", [(a, a ^ 1) for a in range(nrow)])

    def z_shift(x, s):
        return lax.ppermute(x, "row", [(a, (a + 2 * s) % nrow) for a in range(nrow)])

    def col_shift(x, t):
        return lax.ppermute(x, "col", [(a, (a + t) % ncol) for a in range(ncol)])

    def vec_shift(x, t):
        return lax.ppermute(x, "vec", [(a, (a + t) % nvec) for a in range(nvec)])

    row_x = [vectors] + [col_shift(vectors, t) for t in range(1, ncol)]
    ring_x = [z_shift(vectors, s) for s in range(1, nz)]

    def tables(count):
        shape = pltpu.VMEM((count + 1, 2 * vlocal, tile), vectors.dtype)
        return [shape, shape]

    def sums(count):
        return [pltpu.VMEM((count, vlocal, tile), F32)] * 2

    block = jax.ShapeDtypeStruct((vlocal, width), F32)
    ring = jax.ShapeDtypeStruct((vlocal, nz * width), F32)
    step = (nz, ncol, stretch)
    cost = pl.CostEstimate(
        flops=2 * slots * tile * tile * 2 * vlocal, bytes_accessed=slots * tile * tile * 2, transcendentals=0
    )
    lists = [pltpu.VMEM((2, slots), jnp.int32), pltpu.SMEM((2, slots), jnp.int32)]
    mine, other, x, wide = pl.pallas_call(
        functools.partial(mirror_kernel, step),
        out_shape=[ring, ring, jax.ShapeDtypeStruct(vectors.shape, vectors.dtype), jax.ShapeDtypeStruct((vlocal, LONGER * ncol * width), vectors.dtype)],
        in_specs=[SMEM] + [VMEM] * 3 + [HBM] + [VMEM] * ncol,
        out_specs=[VMEM] * 4,
        scratch_shapes=lists
        + [pltpu.SemaphoreType.DMA((2,))]
        + tables(span)
        + sums(nrow * stretch),
        compiler_params=params(6),
        cost_estimate=cost,
        name="mirror",
    )(tile_counts, rows, cols, tiles, x_hbm, token, *row_x[1:])
    near = jnp.concatenate([x] + ring_x, axis=1)
    far = core_swap(near)
    theirs = core_swap(other)
    pieces = pl.pallas_call(
        functools.partial(pair_kernel, nz),
        out_shape=[block] * nz,
        in_specs=[VMEM] * 2,
        out_specs=[VMEM] * nz,
        compiler_params=params(6),
        name="pair",
    )(mine, theirs)
    col_parts = [pieces[0]] + [z_shift(pieces[s], s) for s in range(1, nz)]
    row_parts = pl.pallas_call(
        functools.partial(forward_kernel, step),
        out_shape=[block] * ncol,
        in_specs=[SMEM] + [VMEM] * 5,
        out_specs=[VMEM] * ncol,
        scratch_shapes=lists + [pltpu.SemaphoreType.DMA] + tables(nrow * stretch) + sums(span),
        compiler_params=params(6),
        cost_estimate=cost,
        name="forward",
    )(tile_counts, rows, cols, tiles, near, far)
    every_x = [wide] + [vec_shift(wide, t) for t in range(1, nvec)]
    pad = -(-nvec * vlocal // tile) * tile
    message = jax.ShapeDtypeStruct((vlocal, width + pad), F32)
    image, share, *messages = pl.pallas_call(
        functools.partial(gram_kernel, nz, ncol, nvec, 1.0 / math.sqrt(width * nrow * ncol)),
        out_shape=[block, jax.ShapeDtypeStruct((vlocal, nvec * vlocal), F32)] + [message] * (ncol - 1),
        in_specs=[VMEM] * (nz + ncol + nvec),
        out_specs=[VMEM] * (ncol + 1),
        compiler_params=params(6),
        name="gram",
    )(*col_parts, *row_parts, *every_x)
    got = jnp.zeros_like(share)
    for t in range(1, ncol):
        message = col_shift(messages[t - 1], t)
        image = image + message[:, :width]
        got = got + message[:, width : width + share.shape[1]]
    share = all_sum(share, got, nz, ncol, messages[0])
    gram = share.T
    return (image.astype(jnp.bfloat16), gram)


def all_sum(share, got, nz, ncol, message):
    if nz * ncol > 8 or nz & (nz - 1) or ncol % 2:
        return lax.psum(share, ("row", "col"))
    nrow = 2 * nz

    def send(x, s, t):
        perm = []
        for a in range(nrow):
            for b in range(ncol):
                perm.append((a * ncol + b, (a ^ (2 * s)) * ncol + (b + t + a % 2) % ncol))
        return lax.ppermute(x, ("row", "col"), perm)

    def swap(x):
        return lax.ppermute(x, "row", [(a, a ^ 1) for a in range(nrow)])

    share = share + swap(message)[:, -(-share.shape[1] // 128) * 128 * -1 :][:, : share.shape[1]]
    for s in range(1, nz):
        for t in range(0, ncol, 2):
            got = got + send(share, s, t)
    return share + got + swap(got)


def solution(mesh):
    assert mesh.shape["row"] % 2 == 0
    sizes = (mesh.shape["row"] // 2, mesh.shape["col"], mesh.shape["vec"])
    return jax.shard_map(
        functools.partial(shards, sizes),
        mesh=mesh,
        in_specs=(
            P("vec", ("row", "col")),
            P("row", "col", None, None, None),
            P("row", "col", None),
            P("row", "col", None),
            P("row", "col"),
        ),
        out_specs=(P("vec", ("row", "col")), P(None, "vec")),
        check_vma=False,
    )
```

```python
import functools
import math

import jax
import jax.numpy as jnp
from jax import lax
from jax.experimental import pallas as pl
from jax.experimental.pallas import tpu as pltpu
from jax.sharding import PartitionSpec as P

UNROLL = 128
LONGER = 4
GROUP = 8
VMEM = pl.BlockSpec(memory_space=pltpu.VMEM)
SMEM = pl.BlockSpec(memory_space=pltpu.SMEM)
HBM = pl.BlockSpec(memory_space=pltpu.HBM)
F32 = jnp.float32
HIGHEST = lax.Precision.HIGHEST


def params(mib):
    return pltpu.CompilerParams(vmem_limit_bytes=mib * 2**20)


def place_block(low, high, block, first, stretch, tile):
    vlocal = block.shape[0]
    zero = jnp.zeros((vlocal, tile), block.dtype)
    for q in range(stretch):
        part = block[:, q * tile : (q + 1) * tile]
        low[first + q] = jnp.concatenate([part, zero], axis=0)
        high[first + q] = jnp.concatenate([zero, part], axis=0)


def multiply_tiles(pick, forward, many, count, tiles, low, high, sums):
    slots = tiles.shape[0]
    tile = tiles.shape[-1]
    vlocal = sums[0].shape[1]
    for acc in sums:
        acc[...] = jnp.zeros_like(acc)

    def chunk(step, carry):
        for g in range(many // (2 * GROUP)):
            results = []
            for u in range(GROUP):
                s = step * many + g * 2 * GROUP + 2 * u
                in0, out0 = pick(s)
                in1, out1 = pick(s + 1)
                left = jnp.concatenate([low[in0], high[in1]], axis=1)
                if forward:
                    right = jnp.concatenate([tiles[s], tiles[s + 1]], axis=1)
                    dims = (((1,), (1,)), ((), ()))
                else:
                    right = tiles[pl.ds(s, 2)].reshape(2 * tile, tile)
                    dims = (((1,), (0,)), ((), ()))
                both = lax.dot_general(left, right, dims, preferred_element_type=F32)
                results.append((both, out0, out1))
            for u, (both, out0, out1) in enumerate(results):
                a, b = sums[(2 * u) % len(sums)], sums[(2 * u + 1) % len(sums)]
                a[out0] += both[:vlocal]
                b[out1] += both[vlocal:]
        return carry

    assert slots % many == 0
    lax.fori_loop(0, pl.cdiv(count, many), chunk, 0)


def divide(x, n):
    if n & (n - 1):
        return lax.div(x, n), lax.rem(x, n)
    return x >> (n.bit_length() - 1), x & (n - 1)


def places(rows, cols, span, stretch):
    group, inner = divide(cols[...], span)
    return divide(rows[...], span)[1], group * stretch + divide(inner, stretch)[1]


def hand_scalars(held, sem, *lists):
    vector, scalar = held
    for n, values in enumerate(lists):
        vector[n : n + 1, :] = values
    copy = pltpu.make_async_copy(vector, scalar, sem)
    copy.start()
    return copy


def position():
    i = lax.axis_index("row")
    return lax.div(i, 2), lax.rem(i, 2), lax.axis_index("col")


def stage_kernel(tiles, token):
    token[...] = jnp.zeros_like(token)


def mirror_kernel(sizes, counts, rows, cols, tiles, x_hbm, token, sibling, *refs):
    nz, ncol, stretch = sizes
    span = ncol * stretch
    blocks, (mine, other, x, wide), refs = refs[: ncol - 1], refs[ncol - 1 : ncol + 3], refs[ncol + 3 :]
    vector, scalar, sems, low, high, *sums = refs
    tile = tiles.shape[-1]
    width = stretch * tile
    count = counts[0, 0]
    own = pltpu.make_async_copy(x_hbm, x, sems.at[0])
    own.start()
    slot = lax.broadcasted_iota(jnp.int32, rows.shape, 1)
    row_place, col_place = places(rows, cols, span, stretch)
    used = jnp.where((slot < count) & (rows[...] != cols[...]), row_place, span)
    indices = hand_scalars((vector, scalar), sems.at[1], used, col_place)
    z, core, j = position()
    for t in range(1, ncol):
        wide[:, t * width : (t + 1) * width] = blocks[t - 1][...]
        place_block(low, high, blocks[t - 1], lax.rem(j + ncol - t, ncol) * stretch, stretch, tile)
    own.wait()
    wide[:, :width] = x[...]
    wide[:, ncol * width : (ncol + 1) * width] = sibling[...]
    wide[:, (ncol + 1) * width :] = jnp.zeros_like(wide[:, (ncol + 1) * width :])
    place_block(low, high, x, j * stretch, stretch, tile)
    low[span] = jnp.zeros(low.shape[1:], low.dtype)
    high[span] = jnp.zeros(high.shape[1:], high.dtype)
    indices.wait()

    def pick(s):
        return scalar[0, s], scalar[1, s]

    multiply_tiles(pick, False, UNROLL, count, tiles, low, high, sums)
    for out, c in ((mine, core), (other, 1 - core)):
        wanted = [(z, c)]
        for p in range((nz - 2) // 2):
            wanted += [(z + nz - (2 * p + 1 + c), 0), (z + nz - (2 * p + 1 + c), 1)]
        wanted += [(z + 1, c)]
        for n, (to, half) in enumerate(wanted):
            for q in range(stretch):
                at = (2 * lax.rem(to, nz) + half) * stretch + q
                total = sums[0][at]
                for acc in sums[1:]:
                    total += acc[at]
                out[:, n * width + q * tile : n * width + (q + 1) * tile] = total


def forward_kernel(sizes, counts, rows, cols, tiles, near, far, *refs):
    nz, ncol, stretch = sizes
    span = ncol * stretch
    outs, (vector, scalar, sem, low, high, *sums) = refs[:ncol], refs[ncol:]
    dead = 2 * nz * stretch
    slot = lax.broadcasted_iota(jnp.int32, rows.shape, 1)
    row_place, col_place = places(rows, cols, span, stretch)
    indices = hand_scalars((vector, scalar), sem, jnp.where(slot < counts[0, 0], col_place, dead), row_place)
    tile = tiles.shape[-1]
    width = stretch * tile
    z, core, j = position()
    for s in range(nz):
        source = 2 * lax.rem(z + nz - s, nz)
        for ref, c in ((near, core), (far, 1 - core)):
            place_block(low, high, ref[:, s * width : (s + 1) * width], (source + c) * stretch, stretch, tile)
    low[dead] = jnp.zeros(low.shape[1:], low.dtype)
    high[dead] = jnp.zeros(high.shape[1:], high.dtype)
    indices.wait()

    def pick(s):
        return scalar[0, s], scalar[1, s]

    multiply_tiles(pick, True, UNROLL, counts[0, 0], tiles, low, high, sums)
    for t in range(ncol):
        first = lax.rem(j + t, ncol) * stretch
        for q in range(stretch):
            total = sums[0][first + q]
            for acc in sums[1:]:
                total += acc[first + q]
            outs[t][:, q * tile : (q + 1) * tile] = total


def pair_kernel(mine, theirs, *outs):
    first = 0
    for out in outs:
        at = slice(first, first + out.shape[1])
        out[...] = mine[:, at] + theirs[:, at]
        first += out.shape[1]


def gram_kernel(nz, ncol, nvec, scale, *refs):
    cols, doubles, refs = refs[:2], refs[2 : 2 + (nz - 2) // 2], refs[2 + (nz - 2) // 2 :]
    parts, refs = refs[:ncol], refs[ncol:]
    xs, (image, give, share, *messages) = refs[:nvec], refs[nvec:]
    width = image.shape[1]
    core = lax.rem(lax.axis_index("row"), 2)
    kept = pl.ds(pl.multiple_of(core * width, width), width)
    given = pl.ds(pl.multiple_of((1 - core) * width, width), width)
    total = parts[0][...]
    for ref in cols:
        total += ref[...]
    away = jnp.zeros_like(total)
    for ref in doubles:
        total += ref[:, kept]
        away += ref[:, given]
    image[...] = total
    give[...] = away
    terms = jnp.concatenate([total] + [parts[ncol - t][...] for t in range(1, ncol)] + [away], axis=1)
    split = []
    rest = terms
    for _ in range(3):
        part = rest.astype(jnp.bfloat16)
        split.append(part)
        rest = rest - part.astype(F32)
    split = jnp.concatenate(split, axis=0)
    vlocal = terms.shape[0]
    every = jnp.concatenate([ref[:, : terms.shape[1]] for ref in xs], axis=0)
    thirds = lax.dot_general(split, every, (((1,), (1,)), ((), ())), preferred_element_type=F32)
    whole = scale * (thirds[:vlocal] + thirds[vlocal : 2 * vlocal] + thirds[2 * vlocal :])
    products = [whole[:, k * vlocal : (k + 1) * vlocal] for k in range(nvec)]
    me = lax.axis_index("vec")
    for a in range(nvec):
        picked = products[0]
        for k in range(1, nvec):
            picked = jnp.where(lax.rem(me + nvec - a, nvec) == k, products[k], picked)
        share[:, a * picked.shape[1] : (a + 1) * picked.shape[1]] = picked
    for t in range(1, ncol):
        message = messages[t - 1]
        message[:, :width] = parts[t][...]
        message[:, width:] = jnp.zeros_like(message[:, width:])
        message[:, width : width + share.shape[1]] = share[...]


def shards(sizes, vectors, tile_vals, tile_rows, tile_cols, tile_counts):
    nz, ncol, nvec = sizes
    nrow = 2 * nz
    vlocal, width = vectors.shape
    slots, tile = tile_vals.shape[2], tile_vals.shape[-1]
    stretch = width // tile
    span = ncol * stretch
    x_hbm, tiles_hbm = (
        pltpu.with_memory_space_constraint(a, pltpu.HBM)
        for a in (vectors, tile_vals[0, 0])
    )
    tiles, rows, cols = tile_vals[0, 0], tile_rows[0], tile_cols[0]
    token = pl.pallas_call(
        stage_kernel,
        out_shape=jax.ShapeDtypeStruct((vlocal, tile), F32),
        in_specs=[HBM],
        out_specs=VMEM,
        compiler_params=params(6),
        cost_estimate=pl.CostEstimate(flops=0, bytes_accessed=2 * tile_vals.size * 2, transcendentals=0),
        name="stage",
    )(tiles_hbm)
    vectors, token = lax.optimization_barrier((vectors, token))

    def core_swap(x):
        return lax.ppermute(x, "row", [(a, a ^ 1) for a in range(nrow)])

    def z_shift(x, s):
        return lax.ppermute(x, "row", [(a, (a + 2 * s) % nrow) for a in range(nrow)])

    def col_shift(x, t):
        return lax.ppermute(x, "col", [(a, (a + t) % ncol) for a in range(ncol)])

    def vec_shift(x, t):
        return lax.ppermute(x, "vec", [(a, (a + t) % nvec) for a in range(nvec)])

    row_x = [vectors] + [col_shift(vectors, t) for t in range(1, ncol)]
    sibling = core_swap(vectors)
    ring_x = [z_shift(vectors, s) for s in range(1, nz)]

    def tables(count):
        shape = pltpu.VMEM((count + 1, 2 * vlocal, tile), vectors.dtype)
        return [shape, shape]

    def sums(count):
        return [pltpu.VMEM((count, vlocal, tile), F32)] * 2

    block = jax.ShapeDtypeStruct((vlocal, width), F32)
    ring = jax.ShapeDtypeStruct((vlocal, nz * width), F32)
    step = (nz, ncol, stretch)
    cost = pl.CostEstimate(
        flops=2 * slots * tile * tile * 2 * vlocal, bytes_accessed=slots * tile * tile * 2, transcendentals=0
    )
    lists = [pltpu.VMEM((2, slots), jnp.int32), pltpu.SMEM((2, slots), jnp.int32)]
    mine, other, x, wide = pl.pallas_call(
        functools.partial(mirror_kernel, step),
        out_shape=[ring, ring, jax.ShapeDtypeStruct(vectors.shape, vectors.dtype), jax.ShapeDtypeStruct((vlocal, LONGER * ncol * width), vectors.dtype)],
        in_specs=[SMEM] + [VMEM] * 3 + [HBM] + [VMEM] * (1 + ncol),
        out_specs=[VMEM] * 4,
        scratch_shapes=lists
        + [pltpu.SemaphoreType.DMA((2,))]
        + tables(span)
        + sums(nrow * stretch),
        compiler_params=params(6),
        cost_estimate=cost,
        name="mirror",
    )(tile_counts, rows, cols, tiles, x_hbm, token, sibling, *row_x[1:])
    near = jnp.concatenate([x] + ring_x, axis=1)
    far = core_swap(near)
    theirs = core_swap(other)
    pairs = (nz - 2) // 2
    double = jax.ShapeDtypeStruct((vlocal, 2 * width), F32)
    pieces = pl.pallas_call(
        pair_kernel,
        out_shape=[block] + [double] * pairs + [block],
        in_specs=[VMEM] * 2,
        out_specs=[VMEM] * (pairs + 2),
        compiler_params=params(6),
        name="pair",
    )(mine, theirs)
    last = z_shift(pieces[-1], 1)
    doubles = []
    for p in range(pairs):
        perm = [(a, (a - 2 * (2 * p + 1 + a % 2)) % nrow) for a in range(nrow)]
        doubles.append(lax.ppermute(pieces[1 + p], "row", perm))
    col_parts = [pieces[0], last] + doubles
    row_parts = pl.pallas_call(
        functools.partial(forward_kernel, step),
        out_shape=[block] * ncol,
        in_specs=[SMEM] + [VMEM] * 5,
        out_specs=[VMEM] * ncol,
        scratch_shapes=lists + [pltpu.SemaphoreType.DMA] + tables(nrow * stretch) + sums(span),
        compiler_params=params(6),
        cost_estimate=cost,
        name="forward",
    )(tile_counts, rows, cols, tiles, near, far)
    every_x = [wide] + [vec_shift(wide, t) for t in range(1, nvec)]
    pad = -(-nvec * vlocal // tile) * tile
    message = jax.ShapeDtypeStruct((vlocal, width + pad), F32)
    image, give, share, *messages = pl.pallas_call(
        functools.partial(gram_kernel, nz, ncol, nvec, 1.0 / math.sqrt(width * nrow * ncol)),
        out_shape=[block, block, jax.ShapeDtypeStruct((vlocal, nvec * vlocal), F32)] + [message] * (ncol - 1),
        in_specs=[VMEM] * (2 + pairs + ncol + nvec),
        out_specs=[VMEM] * (ncol + 2),
        compiler_params=params(6),
        name="gram",
    )(*col_parts, *row_parts, *every_x)
    image = image + core_swap(give)
    got = jnp.zeros_like(share)
    for t in range(1, ncol):
        message = col_shift(messages[t - 1], t)
        image = image + message[:, :width]
        got = got + message[:, width : width + share.shape[1]]
    share = all_sum(share, got, nz, ncol, messages[0])
    gram = share.T
    return (image.astype(jnp.bfloat16), gram)


def all_sum(share, got, nz, ncol, message):
    if nz * ncol > 8 or nz & (nz - 1) or ncol % 2:
        return lax.psum(share, ("row", "col"))
    nrow = 2 * nz

    def send(x, s, t):
        perm = []
        for a in range(nrow):
            for b in range(ncol):
                perm.append((a * ncol + b, (a ^ (2 * s)) * ncol + (b + t + a % 2) % ncol))
        return lax.ppermute(x, ("row", "col"), perm)

    def swap(x):
        return lax.ppermute(x, "row", [(a, a ^ 1) for a in range(nrow)])

    share = share + swap(message)[:, -(-share.shape[1] // 128) * 128 * -1 :][:, : share.shape[1]]
    for s in range(1, nz):
        for t in range(0, ncol, 2):
            got = got + send(share, s, t)
    return share + got + swap(got)


def solution(mesh):
    assert mesh.shape["row"] % 4 == 0
    sizes = (mesh.shape["row"] // 2, mesh.shape["col"], mesh.shape["vec"])
    return jax.shard_map(
        functools.partial(shards, sizes),
        mesh=mesh,
        in_specs=(
            P("vec", ("row", "col")),
            P("row", "col", None, None, None),
            P("row", "col", None),
            P("row", "col", None),
            P("row", "col"),
        ),
        out_specs=(P("vec", ("row", "col")), P(None, "vec")),
        check_vma=False,
    )
```

```python
import functools
import math

import jax
import jax.numpy as jnp
from jax import lax
from jax.experimental import pallas as pl
from jax.experimental.pallas import tpu as pltpu
from jax.sharding import PartitionSpec as P

UNROLL = 128
LONGER = 4
GROUP = 8
VMEM = pl.BlockSpec(memory_space=pltpu.VMEM)
SMEM = pl.BlockSpec(memory_space=pltpu.SMEM)
HBM = pl.BlockSpec(memory_space=pltpu.HBM)
F32 = jnp.float32
HIGHEST = lax.Precision.HIGHEST


def params(mib):
    return pltpu.CompilerParams(vmem_limit_bytes=mib * 2**20)


def place_block(low, high, block, first, stretch, tile):
    vlocal = block.shape[0]
    zero = jnp.zeros((vlocal, tile), block.dtype)
    for q in range(stretch):
        part = block[:, q * tile : (q + 1) * tile]
        low[first + q] = jnp.concatenate([part, zero], axis=0)
        high[first + q] = jnp.concatenate([zero, part], axis=0)


def multiply_tiles(pick, forward, many, count, tiles, low, high, sums):
    slots = tiles.shape[0]
    tile = tiles.shape[-1]
    vlocal = sums[0].shape[1]
    for acc in sums:
        acc[...] = jnp.zeros_like(acc)

    def chunk(step, carry):
        for g in range(many // (2 * GROUP)):
            results = []
            for u in range(GROUP):
                s = step * many + g * 2 * GROUP + 2 * u
                in0, out0 = pick(s)
                in1, out1 = pick(s + 1)
                left = jnp.concatenate([low[in0], high[in1]], axis=1)
                if forward:
                    right = jnp.concatenate([tiles[s], tiles[s + 1]], axis=1)
                    dims = (((1,), (1,)), ((), ()))
                else:
                    right = tiles[pl.ds(s, 2)].reshape(2 * tile, tile)
                    dims = (((1,), (0,)), ((), ()))
                both = lax.dot_general(left, right, dims, preferred_element_type=F32)
                results.append((both, out0, out1))
            for u, (both, out0, out1) in enumerate(results):
                a, b = sums[(2 * u) % len(sums)], sums[(2 * u + 1) % len(sums)]
                a[out0] += both[:vlocal]
                b[out1] += both[vlocal:]
        return carry

    assert slots % many == 0
    lax.fori_loop(0, pl.cdiv(count, many), chunk, 0)


def divide(x, n):
    if n & (n - 1):
        return lax.div(x, n), lax.rem(x, n)
    return x >> (n.bit_length() - 1), x & (n - 1)


def places(rows, cols, span, stretch):
    group, inner = divide(cols[...], span)
    return divide(rows[...], span)[1], group * stretch + divide(inner, stretch)[1]


def hand_scalars(held, sem, *lists):
    vector, scalar = held
    for n, values in enumerate(lists):
        vector[n : n + 1, :] = values
    copy = pltpu.make_async_copy(vector, scalar, sem)
    copy.start()
    return copy


def position():
    i = lax.axis_index("row")
    return lax.div(i, 2), lax.rem(i, 2), lax.axis_index("col")


def stage_kernel(tiles, token):
    token[...] = jnp.zeros_like(token)


def mirror_kernel(sizes, counts, rows, cols, tiles, x_hbm, token, sibling, *refs):
    nz, ncol, stretch = sizes
    span = ncol * stretch
    blocks, (mine, other, x, wide), refs = refs[: ncol - 1], refs[ncol - 1 : ncol + 3], refs[ncol + 3 :]
    vector, scalar, sems, low, high, *sums = refs
    tile = tiles.shape[-1]
    width = stretch * tile
    count = counts[0, 0]
    own = pltpu.make_async_copy(x_hbm, x, sems.at[0])
    own.start()
    slot = lax.broadcasted_iota(jnp.int32, rows.shape, 1)
    row_place, col_place = places(rows, cols, span, stretch)
    used = jnp.where((slot < count) & (rows[...] != cols[...]), row_place, span)
    indices = hand_scalars((vector, scalar), sems.at[1], used, col_place)
    z, core, j = position()
    for t in range(1, ncol):
        wide[:, t * width : (t + 1) * width] = blocks[t - 1][...]
        place_block(low, high, blocks[t - 1], lax.rem(j + ncol - t, ncol) * stretch, stretch, tile)
    own.wait()
    wide[:, :width] = x[...]
    wide[:, ncol * width : (ncol + 1) * width] = sibling[...]
    wide[:, (ncol + 1) * width :] = jnp.zeros_like(wide[:, (ncol + 1) * width :])
    place_block(low, high, x, j * stretch, stretch, tile)
    low[span] = jnp.zeros(low.shape[1:], low.dtype)
    high[span] = jnp.zeros(high.shape[1:], high.dtype)
    indices.wait()

    def pick(s):
        return scalar[0, s], scalar[1, s]

    multiply_tiles(pick, False, UNROLL, count, tiles, low, high, sums)
    for out, c in ((mine, core), (other, 1 - core)):
        wanted = [(z, c)]
        for p in range((nz - 2) // 2):
            wanted += [(z + nz - (2 * p + 2 - c), 0), (z + nz - (2 * p + 2 - c), 1)]
        wanted += [(z + 1, c)]
        for n, (to, half) in enumerate(wanted):
            for q in range(stretch):
                at = (2 * lax.rem(to, nz) + half) * stretch + q
                total = sums[0][at]
                for acc in sums[1:]:
                    total += acc[at]
                out[:, n * width + q * tile : n * width + (q + 1) * tile] = total


def forward_kernel(sizes, counts, rows, cols, tiles, near, far, *refs):
    nz, ncol, stretch = sizes
    span = ncol * stretch
    outs, (vector, scalar, sem, low, high, *sums) = refs[:ncol], refs[ncol:]
    dead = 2 * nz * stretch
    slot = lax.broadcasted_iota(jnp.int32, rows.shape, 1)
    row_place, col_place = places(rows, cols, span, stretch)
    indices = hand_scalars((vector, scalar), sem, jnp.where(slot < counts[0, 0], col_place, dead), row_place)
    tile = tiles.shape[-1]
    width = stretch * tile
    z, core, j = position()
    for s in range(nz):
        source = 2 * lax.rem(z + nz - s, nz)
        for ref, c in ((near, core), (far, 1 - core)):
            place_block(low, high, ref[:, s * width : (s + 1) * width], (source + c) * stretch, stretch, tile)
    low[dead] = jnp.zeros(low.shape[1:], low.dtype)
    high[dead] = jnp.zeros(high.shape[1:], high.dtype)
    indices.wait()

    def pick(s):
        return scalar[0, s], scalar[1, s]

    multiply_tiles(pick, True, UNROLL, counts[0, 0], tiles, low, high, sums)
    for t in range(ncol):
        first = lax.rem(j + t, ncol) * stretch
        for q in range(stretch):
            total = sums[0][first + q]
            for acc in sums[1:]:
                total += acc[first + q]
            outs[t][:, q * tile : (q + 1) * tile] = total


def pair_kernel(mine, theirs, *outs):
    first = 0
    for out in outs:
        at = slice(first, first + out.shape[1])
        out[...] = mine[:, at] + theirs[:, at]
        first += out.shape[1]


def gram_kernel(nz, ncol, nvec, scale, *refs):
    cols, doubles, refs = refs[:2], refs[2 : 2 + (nz - 2) // 2], refs[2 + (nz - 2) // 2 :]
    parts, refs = refs[:ncol], refs[ncol:]
    xs, (image, share, give, *messages) = refs[:nvec], refs[nvec:]
    width = image.shape[1]
    core = lax.rem(lax.axis_index("row"), 2)
    kept = pl.ds(pl.multiple_of(core * width, width), width)
    given = pl.ds(pl.multiple_of((1 - core) * width, width), width)
    total = parts[0][...]
    for ref in cols:
        total += ref[...]
    away = jnp.zeros_like(total)
    for ref in doubles:
        total += ref[:, kept]
        away += ref[:, given]
    image[...] = total
    terms = jnp.concatenate([total] + [parts[ncol - t][...] for t in range(1, ncol)] + [away], axis=1)
    split = []
    rest = terms
    for _ in range(3):
        part = rest.astype(jnp.bfloat16)
        split.append(part)
        rest = rest - part.astype(F32)
    split = jnp.concatenate(split, axis=0)
    vlocal = terms.shape[0]
    every = jnp.concatenate([ref[:, : terms.shape[1]] for ref in xs], axis=0)
    thirds = lax.dot_general(split, every, (((1,), (1,)), ((), ())), preferred_element_type=F32)
    whole = scale * (thirds[:vlocal] + thirds[vlocal : 2 * vlocal] + thirds[2 * vlocal :])
    products = [whole[:, k * vlocal : (k + 1) * vlocal] for k in range(nvec)]
    me = lax.axis_index("vec")
    for a in range(nvec):
        picked = products[0]
        for k in range(1, nvec):
            picked = jnp.where(lax.rem(me + nvec - a, nvec) == k, products[k], picked)
        share[:, a * picked.shape[1] : (a + 1) * picked.shape[1]] = picked
    for message, rows in zip((give, *messages), (away, *(ref[...] for ref in parts[1:]))):
        message[:, :width] = rows
        message[:, width:] = jnp.zeros_like(message[:, width:])
        message[:, width : width + share.shape[1]] = share[...]


def shards(sizes, vectors, tile_vals, tile_rows, tile_cols, tile_counts):
    nz, ncol, nvec = sizes
    nrow = 2 * nz
    vlocal, width = vectors.shape
    slots, tile = tile_vals.shape[2], tile_vals.shape[-1]
    stretch = width // tile
    span = ncol * stretch
    x_hbm, tiles_hbm = (
        pltpu.with_memory_space_constraint(a, pltpu.HBM)
        for a in (vectors, tile_vals[0, 0])
    )
    tiles, rows, cols = tile_vals[0, 0], tile_rows[0], tile_cols[0]
    token = pl.pallas_call(
        stage_kernel,
        out_shape=jax.ShapeDtypeStruct((vlocal, tile), F32),
        in_specs=[HBM],
        out_specs=VMEM,
        compiler_params=params(6),
        cost_estimate=pl.CostEstimate(flops=0, bytes_accessed=2 * tile_vals.size * 2, transcendentals=0),
        name="stage",
    )(tiles_hbm)
    vectors, token = lax.optimization_barrier((vectors, token))

    def core_swap(x):
        return lax.ppermute(x, "row", [(a, a ^ 1) for a in range(nrow)])

    def z_shift(x, s):
        return lax.ppermute(x, "row", [(a, (a + 2 * s) % nrow) for a in range(nrow)])

    def col_shift(x, t):
        return lax.ppermute(x, "col", [(a, (a + t) % ncol) for a in range(ncol)])

    def vec_shift(x, t):
        return lax.ppermute(x, "vec", [(a, (a + t) % nvec) for a in range(nvec)])

    row_x = [vectors] + [col_shift(vectors, t) for t in range(1, ncol)]
    sibling = core_swap(vectors)
    ring_x = [z_shift(vectors, s) for s in range(1, nz)]

    def tables(count):
        shape = pltpu.VMEM((count + 1, 2 * vlocal, tile), vectors.dtype)
        return [shape, shape]

    def sums(count):
        return [pltpu.VMEM((count, vlocal, tile), F32)] * 2

    block = jax.ShapeDtypeStruct((vlocal, width), F32)
    ring = jax.ShapeDtypeStruct((vlocal, nz * width), F32)
    step = (nz, ncol, stretch)
    cost = pl.CostEstimate(
        flops=2 * slots * tile * tile * 2 * vlocal, bytes_accessed=slots * tile * tile * 2, transcendentals=0
    )
    lists = [pltpu.VMEM((2, slots), jnp.int32), pltpu.SMEM((2, slots), jnp.int32)]
    mine, other, x, wide = pl.pallas_call(
        functools.partial(mirror_kernel, step),
        out_shape=[ring, ring, jax.ShapeDtypeStruct(vectors.shape, vectors.dtype), jax.ShapeDtypeStruct((vlocal, LONGER * ncol * width), vectors.dtype)],
        in_specs=[SMEM] + [VMEM] * 3 + [HBM] + [VMEM] * (1 + ncol),
        out_specs=[VMEM] * 4,
        scratch_shapes=lists
        + [pltpu.SemaphoreType.DMA((2,))]
        + tables(span)
        + sums(nrow * stretch),
        compiler_params=params(6),
        cost_estimate=cost,
        name="mirror",
    )(tile_counts, rows, cols, tiles, x_hbm, token, sibling, *row_x[1:])
    near = jnp.concatenate([x] + ring_x, axis=1)
    far = core_swap(near)
    theirs = core_swap(other)
    pairs = (nz - 2) // 2
    double = jax.ShapeDtypeStruct((vlocal, 2 * width), F32)
    pieces = pl.pallas_call(
        pair_kernel,
        out_shape=[block] + [double] * pairs + [block],
        in_specs=[VMEM] * 2,
        out_specs=[VMEM] * (pairs + 2),
        compiler_params=params(6),
        name="pair",
    )(mine, theirs)
    last = z_shift(pieces[-1], 1)
    doubles = []
    for p in range(pairs):
        perm = [(a, (a - 2 * (2 * p + 2 - a % 2)) % nrow) for a in range(nrow)]
        doubles.append(lax.ppermute(pieces[1 + p], "row", perm))
    col_parts = [pieces[0], last] + doubles
    row_parts = pl.pallas_call(
        functools.partial(forward_kernel, step),
        out_shape=[block] * ncol,
        in_specs=[SMEM] + [VMEM] * 5,
        out_specs=[VMEM] * ncol,
        scratch_shapes=lists + [pltpu.SemaphoreType.DMA] + tables(nrow * stretch) + sums(span),
        compiler_params=params(6),
        cost_estimate=cost,
        name="forward",
    )(tile_counts, rows, cols, tiles, near, far)
    every_x = [wide] + [vec_shift(wide, t) for t in range(1, nvec)]
    pad = -(-nvec * vlocal // tile) * tile
    message = jax.ShapeDtypeStruct((vlocal, width + pad), F32)
    image, share, give, *messages = pl.pallas_call(
        functools.partial(gram_kernel, nz, ncol, nvec, 1.0 / math.sqrt(width * nrow * ncol)),
        out_shape=[block, jax.ShapeDtypeStruct((vlocal, nvec * vlocal), F32)] + [message] * ncol,
        in_specs=[VMEM] * (2 + pairs + ncol + nvec),
        out_specs=[VMEM] * (ncol + 2),
        compiler_params=params(6),
        name="gram",
    )(*col_parts, *row_parts, *every_x)
    swapped = core_swap(give)
    image = image + swapped[:, :width]
    share = share + swapped[:, width : width + share.shape[1]]
    got = jnp.zeros_like(share)
    for t in range(1, ncol):
        message = col_shift(messages[t - 1], t)
        image = image + message[:, :width]
        got = got + message[:, width : width + share.shape[1]]
    share = all_sum(share, got, nz, ncol)
    gram = share.T
    return (image.astype(jnp.bfloat16), gram)


def all_sum(share, got, nz, ncol):
    if nz * ncol > 8 or nz & (nz - 1) or ncol % 2:
        return 0.5 * lax.psum(share, ("row", "col"))
    nrow = 2 * nz

    def send(x, s, t):
        perm = []
        for a in range(nrow):
            for b in range(ncol):
                perm.append((a * ncol + b, (a ^ (2 * s)) * ncol + (b + t + a % 2) % ncol))
        return lax.ppermute(x, ("row", "col"), perm)

    def swap(x):
        return lax.ppermute(x, "row", [(a, a ^ 1) for a in range(nrow)])

    for s in range(1, nz):
        for t in range(0, ncol, 2):
            got = got + send(share, s, t)
    return share + got + swap(got)


def solution(mesh):
    assert mesh.shape["row"] % 4 == 0
    sizes = (mesh.shape["row"] // 2, mesh.shape["col"], mesh.shape["vec"])
    return jax.shard_map(
        functools.partial(shards, sizes),
        mesh=mesh,
        in_specs=(
            P("vec", ("row", "col")),
            P("row", "col", None, None, None),
            P("row", "col", None),
            P("row", "col", None),
            P("row", "col"),
        ),
        out_specs=(P("vec", ("row", "col")), P(None, "vec")),
        check_vma=False,
    )
```

```python
import functools
import math

import jax
import jax.numpy as jnp
from jax import lax
from jax.experimental import pallas as pl
from jax.experimental.pallas import tpu as pltpu
from jax.sharding import PartitionSpec as P

UNROLL = 128
LONGER = 4
GROUP = 8
VMEM = pl.BlockSpec(memory_space=pltpu.VMEM)
SMEM = pl.BlockSpec(memory_space=pltpu.SMEM)
HBM = pl.BlockSpec(memory_space=pltpu.HBM)
F32 = jnp.float32
HIGHEST = lax.Precision.HIGHEST


def params(mib):
    return pltpu.CompilerParams(vmem_limit_bytes=mib * 2**20)


def place_block(low, high, block, first, stretch, tile):
    vlocal = block.shape[0]
    zero = jnp.zeros((vlocal, tile), block.dtype)
    for q in range(stretch):
        part = block[:, q * tile : (q + 1) * tile]
        low[first + q] = jnp.concatenate([part, zero], axis=0)
        high[first + q] = jnp.concatenate([zero, part], axis=0)


def multiply_tiles(pick, forward, many, count, tiles, low, high, sums):
    slots = tiles.shape[0]
    tile = tiles.shape[-1]
    vlocal = sums[0].shape[1]
    for acc in sums:
        acc[...] = jnp.zeros_like(acc)

    def chunk(step, carry):
        for g in range(many // (2 * GROUP)):
            results = []
            for u in range(GROUP):
                s = step * many + g * 2 * GROUP + 2 * u
                in0, out0 = pick(s)
                in1, out1 = pick(s + 1)
                left = jnp.concatenate([low[in0], high[in1]], axis=1)
                if forward:
                    right = jnp.concatenate([tiles[s], tiles[s + 1]], axis=1)
                    dims = (((1,), (1,)), ((), ()))
                else:
                    right = tiles[pl.ds(s, 2)].reshape(2 * tile, tile)
                    dims = (((1,), (0,)), ((), ()))
                both = lax.dot_general(left, right, dims, preferred_element_type=F32)
                results.append((both, out0, out1))
            for u, (both, out0, out1) in enumerate(results):
                a, b = sums[(2 * u) % len(sums)], sums[(2 * u + 1) % len(sums)]
                a[out0] += both[:vlocal]
                b[out1] += both[vlocal:]
        return carry

    assert slots % many == 0
    lax.fori_loop(0, pl.cdiv(count, many), chunk, 0)


def divide(x, n):
    if n & (n - 1):
        return lax.div(x, n), lax.rem(x, n)
    return x >> (n.bit_length() - 1), x & (n - 1)


def places(rows, cols, span, stretch):
    group, inner = divide(cols[...], span)
    return divide(rows[...], span)[1], group * stretch + divide(inner, stretch)[1]


def hand_scalars(held, sem, *lists):
    vector, scalar = held
    for n, values in enumerate(lists):
        vector[n : n + 1, :] = values
    copy = pltpu.make_async_copy(vector, scalar, sem)
    copy.start()
    return copy


def position():
    i = lax.axis_index("row")
    return lax.div(i, 2), lax.rem(i, 2), lax.axis_index("col")


def stage_kernel(tiles, token):
    token[...] = jnp.zeros_like(token)


def mirror_kernel(sizes, counts, rows, cols, tiles, x, token, sibling, *refs):
    nz, ncol, stretch = sizes
    span = ncol * stretch
    blocks, (mine, other, own, wide), refs = refs[: ncol - 1], refs[ncol - 1 : ncol + 3], refs[ncol + 3 :]
    vector, scalar, sem, low, high, *sums = refs
    tile = tiles.shape[-1]
    width = stretch * tile
    count = counts[0, 0]
    slot = lax.broadcasted_iota(jnp.int32, rows.shape, 1)
    row_place, col_place = places(rows, cols, span, stretch)
    used = jnp.where((slot < count) & (rows[...] != cols[...]), row_place, span)
    indices = hand_scalars((vector, scalar), sem, used, col_place)
    z, core, j = position()
    for t in range(1, ncol):
        wide[:, t * width : (t + 1) * width] = blocks[t - 1][...]
        place_block(low, high, blocks[t - 1], lax.rem(j + ncol - t, ncol) * stretch, stretch, tile)
    own[...] = x[...]
    wide[:, :width] = x[...]
    wide[:, ncol * width : (ncol + 1) * width] = sibling[...]
    wide[:, (ncol + 1) * width :] = jnp.zeros_like(wide[:, (ncol + 1) * width :])
    place_block(low, high, x, j * stretch, stretch, tile)
    low[span] = jnp.zeros(low.shape[1:], low.dtype)
    high[span] = jnp.zeros(high.shape[1:], high.dtype)
    indices.wait()

    def pick(s):
        return scalar[0, s], scalar[1, s]

    multiply_tiles(pick, False, UNROLL, count, tiles, low, high, sums)
    for out, c in ((mine, core), (other, 1 - core)):
        wanted = [(z, c)]
        for p in range((nz - 2) // 2):
            wanted += [(z + nz - (2 * p + 2 - c), 0), (z + nz - (2 * p + 2 - c), 1)]
        wanted += [(z + 1, c)]
        for n, (to, half) in enumerate(wanted):
            for q in range(stretch):
                at = (2 * lax.rem(to, nz) + half) * stretch + q
                total = sums[0][at]
                for acc in sums[1:]:
                    total += acc[at]
                out[:, n * width + q * tile : n * width + (q + 1) * tile] = total


def forward_kernel(sizes, counts, rows, cols, tiles, near, far, *refs):
    nz, ncol, stretch = sizes
    span = ncol * stretch
    outs, (vector, scalar, sem, low, high, *sums) = refs[:ncol], refs[ncol:]
    dead = 2 * nz * stretch
    slot = lax.broadcasted_iota(jnp.int32, rows.shape, 1)
    row_place, col_place = places(rows, cols, span, stretch)
    indices = hand_scalars((vector, scalar), sem, jnp.where(slot < counts[0, 0], col_place, dead), row_place)
    tile = tiles.shape[-1]
    width = stretch * tile
    z, core, j = position()
    for s in range(nz):
        source = 2 * lax.rem(z + nz - s, nz)
        for ref, c in ((near, core), (far, 1 - core)):
            place_block(low, high, ref[:, s * width : (s + 1) * width], (source + c) * stretch, stretch, tile)
    low[dead] = jnp.zeros(low.shape[1:], low.dtype)
    high[dead] = jnp.zeros(high.shape[1:], high.dtype)
    indices.wait()

    def pick(s):
        return scalar[0, s], scalar[1, s]

    multiply_tiles(pick, True, UNROLL, counts[0, 0], tiles, low, high, sums)
    for t in range(ncol):
        first = lax.rem(j + t, ncol) * stretch
        for q in range(stretch):
            total = sums[0][first + q]
            for acc in sums[1:]:
                total += acc[first + q]
            outs[t][:, q * tile : (q + 1) * tile] = total


def pair_kernel(mine, theirs, *outs):
    first = 0
    for out in outs:
        at = slice(first, first + out.shape[1])
        out[...] = mine[:, at] + theirs[:, at]
        first += out.shape[1]


def gram_kernel(nz, ncol, nvec, scale, *refs):
    cols, doubles, refs = refs[:2], refs[2 : 2 + (nz - 2) // 2], refs[2 + (nz - 2) // 2 :]
    parts, refs = refs[:ncol], refs[ncol:]
    xs, (image, share, give, *messages) = refs[:nvec], refs[nvec:]
    width = image.shape[1]
    core = lax.rem(lax.axis_index("row"), 2)
    kept = pl.ds(pl.multiple_of(core * width, width), width)
    given = pl.ds(pl.multiple_of((1 - core) * width, width), width)
    total = parts[0][...]
    for ref in cols:
        total += ref[...]
    away = jnp.zeros_like(total)
    for ref in doubles:
        total += ref[:, kept]
        away += ref[:, given]
    image[...] = total
    terms = jnp.concatenate([total] + [parts[ncol - t][...] for t in range(1, ncol)] + [away], axis=1)
    split = []
    rest = terms
    for _ in range(3):
        part = rest.astype(jnp.bfloat16)
        split.append(part)
        rest = rest - part.astype(F32)
    split = jnp.concatenate(split, axis=0)
    vlocal = terms.shape[0]
    every = jnp.concatenate([ref[:, : terms.shape[1]] for ref in xs], axis=0)
    thirds = lax.dot_general(split, every, (((1,), (1,)), ((), ())), preferred_element_type=F32)
    whole = scale * (thirds[:vlocal] + thirds[vlocal : 2 * vlocal] + thirds[2 * vlocal :])
    products = [whole[:, k * vlocal : (k + 1) * vlocal] for k in range(nvec)]
    me = lax.axis_index("vec")
    for a in range(nvec):
        picked = products[0]
        for k in range(1, nvec):
            picked = jnp.where(lax.rem(me + nvec - a, nvec) == k, products[k], picked)
        share[:, a * picked.shape[1] : (a + 1) * picked.shape[1]] = picked
    for message, rows in zip((give, *messages), (away, *(ref[...] for ref in parts[1:]))):
        message[:, :width] = rows
        message[:, width:] = jnp.zeros_like(message[:, width:])
        message[:, width : width + share.shape[1]] = share[...]


def shards(sizes, vectors, tile_vals, tile_rows, tile_cols, tile_counts):
    nz, ncol, nvec = sizes
    nrow = 2 * nz
    vlocal, width = vectors.shape
    slots, tile = tile_vals.shape[2], tile_vals.shape[-1]
    stretch = width // tile
    span = ncol * stretch
    tiles_hbm = pltpu.with_memory_space_constraint(tile_vals[0, 0], pltpu.HBM)
    tiles, rows, cols = tile_vals[0, 0], tile_rows[0], tile_cols[0]
    token = pl.pallas_call(
        stage_kernel,
        out_shape=jax.ShapeDtypeStruct((vlocal, tile), F32),
        in_specs=[HBM],
        out_specs=VMEM,
        compiler_params=params(6),
        cost_estimate=pl.CostEstimate(flops=0, bytes_accessed=2 * tile_vals.size * 2, transcendentals=0),
        name="stage",
    )(tiles_hbm)
    vectors, token = lax.optimization_barrier((vectors, token))

    def core_swap(x):
        return lax.ppermute(x, "row", [(a, a ^ 1) for a in range(nrow)])

    def z_shift(x, s):
        return lax.ppermute(x, "row", [(a, (a + 2 * s) % nrow) for a in range(nrow)])

    def col_shift(x, t):
        return lax.ppermute(x, "col", [(a, (a + t) % ncol) for a in range(ncol)])

    def vec_shift(x, t):
        return lax.ppermute(x, "vec", [(a, (a + t) % nvec) for a in range(nvec)])

    row_x = [vectors] + [col_shift(vectors, t) for t in range(1, ncol)]
    sibling = core_swap(vectors)
    ring_x = [z_shift(vectors, s) for s in range(1, nz)]

    def tables(count):
        shape = pltpu.VMEM((count + 1, 2 * vlocal, tile), vectors.dtype)
        return [shape, shape]

    def sums(count):
        return [pltpu.VMEM((count, vlocal, tile), F32)] * 2

    block = jax.ShapeDtypeStruct((vlocal, width), F32)
    ring = jax.ShapeDtypeStruct((vlocal, nz * width), F32)
    step = (nz, ncol, stretch)
    cost = pl.CostEstimate(
        flops=2 * slots * tile * tile * 2 * vlocal, bytes_accessed=slots * tile * tile * 2, transcendentals=0
    )
    lists = [pltpu.VMEM((2, slots), jnp.int32), pltpu.SMEM((2, slots), jnp.int32)]
    mine, other, x, wide = pl.pallas_call(
        functools.partial(mirror_kernel, step),
        out_shape=[ring, ring, jax.ShapeDtypeStruct(vectors.shape, vectors.dtype), jax.ShapeDtypeStruct((vlocal, LONGER * ncol * width), vectors.dtype)],
        in_specs=[SMEM] + [VMEM] * 3 + [VMEM] * (2 + ncol),
        out_specs=[VMEM] * 4,
        scratch_shapes=lists
        + [pltpu.SemaphoreType.DMA]
        + tables(span)
        + sums(nrow * stretch),
        compiler_params=params(6),
        cost_estimate=cost,
        name="mirror",
    )(tile_counts, rows, cols, tiles, vectors, token, sibling, *row_x[1:])
    near = jnp.concatenate([x] + ring_x, axis=1)
    far = core_swap(near)
    theirs = core_swap(other)
    pairs = (nz - 2) // 2
    double = jax.ShapeDtypeStruct((vlocal, 2 * width), F32)
    pieces = pl.pallas_call(
        pair_kernel,
        out_shape=[block] + [double] * pairs + [block],
        in_specs=[VMEM] * 2,
        out_specs=[VMEM] * (pairs + 2),
        compiler_params=params(6),
        name="pair",
    )(mine, theirs)
    last = z_shift(pieces[-1], 1)
    doubles = []
    for p in range(pairs):
        perm = [(a, (a - 2 * (2 * p + 2 - a % 2)) % nrow) for a in range(nrow)]
        doubles.append(lax.ppermute(pieces[1 + p], "row", perm))
    col_parts = [pieces[0], last] + doubles
    row_parts = pl.pallas_call(
        functools.partial(forward_kernel, step),
        out_shape=[block] * ncol,
        in_specs=[SMEM] + [VMEM] * 5,
        out_specs=[VMEM] * ncol,
        scratch_shapes=lists + [pltpu.SemaphoreType.DMA] + tables(nrow * stretch) + sums(span),
        compiler_params=params(6),
        cost_estimate=cost,
        name="forward",
    )(tile_counts, rows, cols, tiles, near, far)
    every_x = [wide] + [vec_shift(wide, t) for t in range(1, nvec)]
    pad = -(-nvec * vlocal // tile) * tile
    message = jax.ShapeDtypeStruct((vlocal, width + pad), F32)
    image, share, give, *messages = pl.pallas_call(
        functools.partial(gram_kernel, nz, ncol, nvec, 1.0 / math.sqrt(width * nrow * ncol)),
        out_shape=[block, jax.ShapeDtypeStruct((vlocal, nvec * vlocal), F32)] + [message] * ncol,
        in_specs=[VMEM] * (2 + pairs + ncol + nvec),
        out_specs=[VMEM] * (ncol + 2),
        compiler_params=params(6),
        name="gram",
    )(*col_parts, *row_parts, *every_x)
    swapped = core_swap(give)
    image = image + swapped[:, :width]
    share = share + swapped[:, width : width + share.shape[1]]
    got = jnp.zeros_like(share)
    for t in range(1, ncol):
        message = col_shift(messages[t - 1], t)
        image = image + message[:, :width]
        got = got + message[:, width : width + share.shape[1]]
    share = all_sum(share, got, nz, ncol)
    gram = share.T
    return (image.astype(jnp.bfloat16), gram)


def all_sum(share, got, nz, ncol):
    if nz * ncol > 8 or nz & (nz - 1) or ncol % 2:
        return 0.5 * lax.psum(share, ("row", "col"))
    nrow = 2 * nz

    def send(x, s, t):
        perm = []
        for a in range(nrow):
            for b in range(ncol):
                perm.append((a * ncol + b, (a ^ (2 * s)) * ncol + (b + t + a % 2) % ncol))
        return lax.ppermute(x, ("row", "col"), perm)

    def swap(x):
        return lax.ppermute(x, "row", [(a, a ^ 1) for a in range(nrow)])

    for s in range(1, nz):
        for t in range(0, ncol, 2):
            got = got + send(share, s, t)
    return share + got + swap(got)


def solution(mesh):
    assert mesh.shape["row"] % 4 == 0
    sizes = (mesh.shape["row"] // 2, mesh.shape["col"], mesh.shape["vec"])
    return jax.shard_map(
        functools.partial(shards, sizes),
        mesh=mesh,
        in_specs=(
            P("vec", ("row", "col")),
            P("row", "col", None, None, None),
            P("row", "col", None),
            P("row", "col", None),
            P("row", "col"),
        ),
        out_specs=(P("vec", ("row", "col")), P(None, "vec")),
        check_vma=False,
    )
```

```python
import functools
import math

import jax
import jax.numpy as jnp
from jax import lax
from jax.experimental import pallas as pl
from jax.experimental.pallas import tpu as pltpu
from jax.sharding import PartitionSpec as P

UNROLL = 128
LONGER = 4
GROUP = 8
VMEM = pl.BlockSpec(memory_space=pltpu.VMEM)
SMEM = pl.BlockSpec(memory_space=pltpu.SMEM)
HBM = pl.BlockSpec(memory_space=pltpu.HBM)
F32 = jnp.float32
HIGHEST = lax.Precision.HIGHEST


def params(mib):
    return pltpu.CompilerParams(vmem_limit_bytes=mib * 2**20)


def place_block(low, high, block, first, stretch, tile):
    vlocal = block.shape[0]
    zero = jnp.zeros((vlocal, tile), block.dtype)
    for q in range(stretch):
        part = block[:, q * tile : (q + 1) * tile]
        low[first + q] = jnp.concatenate([part, zero], axis=0)
        high[first + q] = jnp.concatenate([zero, part], axis=0)


def multiply_tiles(pick, forward, many, count, tiles, low, high, sums):
    slots = tiles.shape[0]
    tile = tiles.shape[-1]
    vlocal = sums[0].shape[1]
    for acc in sums:
        acc[...] = jnp.zeros_like(acc)

    def chunk(step, carry):
        for g in range(many // (2 * GROUP)):
            results = []
            for u in range(GROUP):
                s = step * many + g * 2 * GROUP + 2 * u
                in0, out0 = pick(s)
                in1, out1 = pick(s + 1)
                left = jnp.concatenate([low[in0], high[in1]], axis=1)
                if forward:
                    right = jnp.concatenate([tiles[s], tiles[s + 1]], axis=1)
                    dims = (((1,), (1,)), ((), ()))
                else:
                    right = tiles[pl.ds(s, 2)].reshape(2 * tile, tile)
                    dims = (((1,), (0,)), ((), ()))
                both = lax.dot_general(left, right, dims, preferred_element_type=F32)
                results.append((both, out0, out1))
            for u, (both, out0, out1) in enumerate(results):
                a, b = sums[(2 * u) % len(sums)], sums[(2 * u + 1) % len(sums)]
                a[out0] += both[:vlocal]
                b[out1] += both[vlocal:]
        return carry

    assert slots % many == 0
    lax.fori_loop(0, pl.cdiv(count, many), chunk, 0)


def divide(x, n):
    if n & (n - 1):
        return lax.div(x, n), lax.rem(x, n)
    return x >> (n.bit_length() - 1), x & (n - 1)


def places(rows, cols, span, stretch):
    group, inner = divide(cols[...], span)
    return divide(rows[...], span)[1], group * stretch + divide(inner, stretch)[1]


def hand_scalars(held, sem, *lists):
    vector, scalar = held
    for n, values in enumerate(lists):
        vector[n : n + 1, :] = values
    copy = pltpu.make_async_copy(vector, scalar, sem)
    copy.start()
    return copy


def position():
    i = lax.axis_index("row")
    return lax.div(i, 2), lax.rem(i, 2), lax.axis_index("col")


def stage_kernel(tiles, token):
    token[...] = jnp.zeros_like(token)


def mirror_kernel(sizes, counts, rows, cols, tiles, x, token, sibling, *refs):
    nz, ncol, stretch = sizes
    span = ncol * stretch
    blocks, (mine, other, own, wide), refs = refs[: ncol - 1], refs[ncol - 1 : ncol + 3], refs[ncol + 3 :]
    vector, scalar, sem, low, high, *sums = refs
    tile = tiles.shape[-1]
    width = stretch * tile
    count = counts[0, 0]
    slot = lax.broadcasted_iota(jnp.int32, rows.shape, 1)
    row_place, col_place = places(rows, cols, span, stretch)
    used = jnp.where((slot < count) & (rows[...] != cols[...]), row_place, span)
    indices = hand_scalars((vector, scalar), sem, used, col_place)
    z, core, j = position()
    for t in range(1, ncol):
        wide[:, t * width : (t + 1) * width] = blocks[t - 1][...]
        place_block(low, high, blocks[t - 1], lax.rem(j + ncol - t, ncol) * stretch, stretch, tile)
    own[...] = x[...]
    wide[:, :width] = x[...]
    wide[:, ncol * width : (ncol + 1) * width] = sibling[...]
    wide[:, (ncol + 1) * width :] = jnp.zeros_like(wide[:, (ncol + 1) * width :])
    place_block(low, high, x, j * stretch, stretch, tile)
    low[span] = jnp.zeros(low.shape[1:], low.dtype)
    high[span] = jnp.zeros(high.shape[1:], high.dtype)
    indices.wait()

    def pick(s):
        return scalar[0, s], scalar[1, s]

    multiply_tiles(pick, False, UNROLL, count, tiles, low, high, sums)
    for out, c in ((mine, core), (other, 1 - core)):
        wanted = [(z, c)]
        for p in range((nz - 2) // 2):
            wanted += [(z + nz - (2 * p + 2 - c), 0), (z + nz - (2 * p + 2 - c), 1)]
        wanted += [(z + 1, c)]
        for n, (to, half) in enumerate(wanted):
            for q in range(stretch):
                at = (2 * lax.rem(to, nz) + half) * stretch + q
                total = sums[0][at]
                for acc in sums[1:]:
                    total += acc[at]
                out[:, n * width + q * tile : n * width + (q + 1) * tile] = total


def forward_kernel(sizes, counts, rows, cols, tiles, near, far, *refs):
    nz, ncol, stretch = sizes
    span = ncol * stretch
    outs, (vector, scalar, sem, low, high, *sums) = refs[:ncol], refs[ncol:]
    dead = 2 * nz * stretch
    slot = lax.broadcasted_iota(jnp.int32, rows.shape, 1)
    row_place, col_place = places(rows, cols, span, stretch)
    indices = hand_scalars((vector, scalar), sem, jnp.where(slot < counts[0, 0], col_place, dead), row_place)
    tile = tiles.shape[-1]
    width = stretch * tile
    z, core, j = position()
    for s in range(nz):
        source = 2 * lax.rem(z + nz - s, nz)
        for ref, c in ((near, core), (far, 1 - core)):
            place_block(low, high, ref[:, s * width : (s + 1) * width], (source + c) * stretch, stretch, tile)
    low[dead] = jnp.zeros(low.shape[1:], low.dtype)
    high[dead] = jnp.zeros(high.shape[1:], high.dtype)
    indices.wait()

    def pick(s):
        return scalar[0, s], scalar[1, s]

    multiply_tiles(pick, True, UNROLL, counts[0, 0], tiles, low, high, sums)
    for t in range(ncol):
        first = lax.rem(j + t, ncol) * stretch
        for q in range(stretch):
            total = sums[0][first + q]
            for acc in sums[1:]:
                total += acc[first + q]
            outs[t][:, q * tile : (q + 1) * tile] = total


def pair_kernel(mine, theirs, *outs):
    first = 0
    for out in outs:
        at = slice(first, first + out.shape[1])
        out[...] = mine[:, at] + theirs[:, at]
        first += out.shape[1]


def gram_kernel(nz, ncol, nvec, scale, *refs):
    cols, doubles, refs = refs[:2], refs[2 : 2 + (nz - 2) // 2], refs[2 + (nz - 2) // 2 :]
    parts, refs = refs[:ncol], refs[ncol:]
    xs, (image, share, give, *messages) = refs[:nvec], refs[nvec:]
    width = image.shape[1]
    core = lax.rem(lax.axis_index("row"), 2)
    kept = pl.ds(pl.multiple_of(core * width, width), width)
    given = pl.ds(pl.multiple_of((1 - core) * width, width), width)
    total = parts[0][...]
    for ref in cols:
        total += ref[...]
    away = jnp.zeros_like(total)
    for ref in doubles:
        total += ref[:, kept]
        away += ref[:, given]
    image[...] = total
    terms = jnp.concatenate([total] + [parts[ncol - t][...] for t in range(1, ncol)] + [away], axis=1)
    split = []
    rest = terms
    for _ in range(3):
        part = rest.astype(jnp.bfloat16)
        split.append(part)
        rest = rest - part.astype(F32)
    split = jnp.concatenate(split, axis=0)
    vlocal = terms.shape[0]
    every = jnp.concatenate([ref[:, : terms.shape[1]] for ref in xs], axis=0)
    thirds = lax.dot_general(split, every, (((1,), (1,)), ((), ())), preferred_element_type=F32)
    whole = scale * (thirds[:vlocal] + thirds[vlocal : 2 * vlocal] + thirds[2 * vlocal :])
    products = [whole[:, k * vlocal : (k + 1) * vlocal] for k in range(nvec)]
    me = lax.axis_index("vec")
    for a in range(nvec):
        picked = products[0]
        for k in range(1, nvec):
            picked = jnp.where(lax.rem(me + nvec - a, nvec) == k, products[k], picked)
        share[:, a * picked.shape[1] : (a + 1) * picked.shape[1]] = picked
    for message, rows in zip((give, *messages), (away, *(ref[...] for ref in parts[1:]))):
        message[:, :width] = rows
        message[:, width:] = jnp.zeros_like(message[:, width:])
        message[:, width : width + share.shape[1]] = share[...]


def shards(sizes, vectors, tile_vals, tile_rows, tile_cols, tile_counts):
    nz, ncol, nvec = sizes
    nrow = 2 * nz
    vlocal, width = vectors.shape
    slots, tile = tile_vals.shape[2], tile_vals.shape[-1]
    stretch = width // tile
    span = ncol * stretch
    tiles_hbm = pltpu.with_memory_space_constraint(tile_vals[0, 0], pltpu.HBM)
    tiles, rows, cols = tile_vals[0, 0], tile_rows[0], tile_cols[0]
    token = pl.pallas_call(
        stage_kernel,
        out_shape=jax.ShapeDtypeStruct((vlocal, tile), F32),
        in_specs=[HBM],
        out_specs=VMEM,
        compiler_params=params(6),
        cost_estimate=pl.CostEstimate(flops=0, bytes_accessed=2 * tile_vals.size * 2, transcendentals=0),
        name="stage",
    )(tiles_hbm)
    vectors, token = lax.optimization_barrier((vectors, token))

    def core_swap(x):
        return lax.ppermute(x, "row", [(a, a ^ 1) for a in range(nrow)])

    def z_shift(x, s):
        return lax.ppermute(x, "row", [(a, (a + 2 * s) % nrow) for a in range(nrow)])

    def col_shift(x, t):
        return lax.ppermute(x, "col", [(a, (a + t) % ncol) for a in range(ncol)])

    def vec_shift(x, t):
        return lax.ppermute(x, "vec", [(a, (a + t) % nvec) for a in range(nvec)])

    row_x = [vectors] + [col_shift(vectors, t) for t in range(1, ncol)]
    sibling = core_swap(vectors)
    ring_x = [z_shift(vectors, s) for s in range(1, nz)]

    def tables(count):
        shape = pltpu.VMEM((count + 1, 2 * vlocal, tile), vectors.dtype)
        return [shape, shape]

    def sums(count):
        return [pltpu.VMEM((count, vlocal, tile), F32)] * 2

    block = jax.ShapeDtypeStruct((vlocal, width), F32)
    ring = jax.ShapeDtypeStruct((vlocal, nz * width), F32)
    step = (nz, ncol, stretch)
    cost = pl.CostEstimate(
        flops=2 * slots * tile * tile * 2 * vlocal, bytes_accessed=slots * tile * tile * 2, transcendentals=0
    )
    lists = [pltpu.VMEM((2, slots), jnp.int32), pltpu.SMEM((2, slots), jnp.int32)]
    mine, other, x, wide = pl.pallas_call(
        functools.partial(mirror_kernel, step),
        out_shape=[ring, ring, jax.ShapeDtypeStruct(vectors.shape, vectors.dtype), jax.ShapeDtypeStruct((vlocal, LONGER * ncol * width), vectors.dtype)],
        in_specs=[SMEM] + [VMEM] * 3 + [VMEM] * (2 + ncol),
        out_specs=[VMEM] * 4,
        scratch_shapes=lists
        + [pltpu.SemaphoreType.DMA]
        + tables(span)
        + sums(nrow * stretch),
        compiler_params=params(6),
        cost_estimate=cost,
        name="mirror",
    )(tile_counts, rows, cols, tiles, vectors, token, sibling, *row_x[1:])
    near = jnp.concatenate([x] + ring_x, axis=1)
    far = core_swap(near)
    theirs = core_swap(other)
    pairs = (nz - 2) // 2
    double = jax.ShapeDtypeStruct((vlocal, 2 * width), F32)
    pieces = pl.pallas_call(
        pair_kernel,
        out_shape=[block] + [double] * pairs + [block],
        in_specs=[VMEM] * 2,
        out_specs=[VMEM] * (pairs + 2),
        compiler_params=params(6),
        name="pair",
    )(mine, theirs)
    last = z_shift(pieces[-1], 1)
    doubles = []
    for p in range(pairs):
        perm = [(a, (a - 2 * (2 * p + 2 - a % 2)) % nrow) for a in range(nrow)]
        doubles.append(lax.ppermute(pieces[1 + p], "row", perm))
    col_parts = [pieces[0], last] + doubles
    row_parts = pl.pallas_call(
        functools.partial(forward_kernel, step),
        out_shape=[block] * ncol,
        in_specs=[SMEM] + [VMEM] * 5,
        out_specs=[VMEM] * ncol,
        scratch_shapes=lists + [pltpu.SemaphoreType.DMA] + tables(nrow * stretch) + sums(span),
        compiler_params=params(6),
        cost_estimate=cost,
        name="forward",
    )(tile_counts, rows, cols, tiles, near, far)
    every_x = [wide] + [vec_shift(wide, t) for t in range(1, nvec)]
    pad = -(-nvec * vlocal // tile) * tile
    message = jax.ShapeDtypeStruct((vlocal, width + pad), F32)
    image, share, give, *messages = pl.pallas_call(
        functools.partial(gram_kernel, nz, ncol, nvec, 1.0 / math.sqrt(width * nrow * ncol)),
        out_shape=[block, jax.ShapeDtypeStruct((vlocal, nvec * vlocal), F32)] + [message] * ncol,
        in_specs=[VMEM] * (2 + pairs + ncol + nvec),
        out_specs=[VMEM] * (ncol + 2),
        compiler_params=params(6),
        name="gram",
    )(*col_parts, *row_parts, *every_x)
    swapped = core_swap(give)
    image = image + swapped[:, :width]
    share = share + swapped[:, width : width + share.shape[1]]
    got = jnp.zeros_like(share)
    for t in range(1, ncol):
        message = col_shift(messages[t - 1], t)
        image = image + message[:, :width]
        got = got + message[:, width : width + share.shape[1]]
    share = all_sum(share, got, nz, ncol)
    gram = share.T
    return (image.astype(jnp.bfloat16), gram)


def all_sum(share, got, nz, ncol):
    if nz * ncol > 8 or nz & (nz - 1) or ncol % 2:
        return 0.5 * lax.psum(share, ("row", "col"))
    nrow = 2 * nz

    def send(x, s, t):
        perm = []
        for a in range(nrow):
            for b in range(ncol):
                perm.append((a * ncol + b, (a ^ (2 * s)) * ncol + (b + t + a % 2) % ncol))
        return lax.ppermute(x, ("row", "col"), perm)

    def swap(x):
        return lax.ppermute(x, "row", [(a, a ^ 1) for a in range(nrow)])

    for s in [*range(min(2, nz - 1), 0, -1), *range(3, nz)]:
        for t in range(0, ncol, 2):
            got = got + send(share, s, t)
    return share + got + swap(got)


def solution(mesh):
    assert mesh.shape["row"] % 4 == 0
    sizes = (mesh.shape["row"] // 2, mesh.shape["col"], mesh.shape["vec"])
    return jax.shard_map(
        functools.partial(shards, sizes),
        mesh=mesh,
        in_specs=(
            P("vec", ("row", "col")),
            P("row", "col", None, None, None),
            P("row", "col", None),
            P("row", "col", None),
            P("row", "col"),
        ),
        out_specs=(P("vec", ("row", "col")), P(None, "vec")),
        check_vma=False,
    )
```
